128 devices in a mesh: hour: 2 (over core), bus: 16 (over x, y), line: 4 (over z).
Axes of the slice: x: 4, y: 4, z: 4, core: 2. Of those that a mesh axis runs over, the one named last changes fastest.
Arguments:
- ptdf: bfloat16 [19968, 16384], P('line', 'bus'), may hold values from -0.0625 to 0.0625
- units_out: float32 [192, 8, 4096], P('hour', None, 'bus'), may hold values from 0 to 1.5
- load: float32 [192, 8, 16384], P('hour', None, 'bus'), may hold values from -6 to 6
- unit_node: int32 [4096], P('bus'), may hold values from 0 to 16383, as said below
- commit_index: int32 [192, 4096], P('hour', 'bus'), may hold values from 0 to 3
- relax_levels: float32 [4], replicated, may hold values from 0.25 to 1
- line_active: int32 [192, 19968], P('hour', 'line'), may hold values 0 or 1
- line_limit: float32 [19968], P('line'), may hold values from 0.3 to 1.5
- line_weight: float32 [19968], P('line'), may hold values from 0.3 to 3
- ramp_active: int32 [192, 4096], P(None, 'bus'), may hold values 0 or 1
- ramp_limit: float32 [4096], P('bus'), may hold values from 0.05 to 0.4
- ramp_weight: float32 [4096], P('bus'), may hold values from 0.5 to 5
Outputs:
- units_grad: float32 [192, 8, 4096], P('hour', None, 'bus')
The draws below stay inside these ranges and needn't reach their ends.
Inputs may be any that keep to these rules, and one draw needn't show every extreme that they name: `unit_node`: unit g sits at a node n with n // 1024 = g // 256.
All inputs are finite; a program needn't handle non-finite values. No bound on the sum of `line_active` or of `ramp_active` on one device may be relied on, other than what follows from the above.
Results may differ from the reference program's by a relative error of at most 0.0026.
Values may be sent and summed in bfloat16 or wider, within the bound.
A program may use at most 128 MiB of HBM per device.

```python
import math
import jax
import jax.numpy as jnp
from jax import lax

LINES = 19968
NODES = 16384
SCEN = 8
UNITS_DEV = 256
LEVELS = 4
HOURS = 192
UNITS = 4096
N_BUS = 16


def draw_unit_node(key, part):
    key = jax.random.fold_in(key, 11)
    nodes_dev = NODES // N_BUS
    block = jnp.arange(UNITS, dtype=jnp.int32) // UNITS_DEV
    offset = jax.random.randint(key, (UNITS,), 0, nodes_dev, dtype=jnp.int32)
    placed = block * nodes_dev + offset
    placed = placed.at[0].set(0).at[UNITS - 1].set(NODES - 1)
    return placed.astype(jnp.int32)


def set_ends(array, stream_key, least, largest):
    index_at = [jax.random.randint(jax.random.fold_in(stream_key, axis), (), 0, length) for axis, length in enumerate(array.shape)]
    widest = array.shape.index(max(array.shape))
    neighbour = index_at[:widest] + [(index_at[widest] + 1) % array.shape[widest]] + index_at[widest + 1:]
    return array.at[tuple(index_at)].set(least).at[tuple(neighbour)].set(largest)


def with_spikes(result, stream_key, source, target, blocks, factor):
    owner, partner = [(jnp.arange(result.shape[position]) // (result.shape[position] // blocks)).reshape([-1 if axis == position else 1 for axis in range(result.ndim)]) for position in (source, target)]
    chosen = jax.random.permutation(stream_key, blocks)[partner]
    strong = (owner == chosen) | (owner == (partner + blocks // 2) % blocks)
    return jnp.where(strong, factor * result, result)


def shard_levels(own_key, dims, pieces, smallest, high):
    def one(position, parts):
        heights = jax.random.uniform(jax.random.fold_in(jax.random.fold_in(own_key, 6), position), (parts,), jnp.float32, smallest / len(pieces), high / len(pieces))
        return jnp.repeat(jnp.exp(heights), dims[position] // parts).reshape((-1,) + (1,) * (len(dims) - position - 1))

    loudness = one(*pieces[0])
    for cut in pieces[1:]:
        loudness = loudness * one(*cut)
    return loudness


def noise(own_key, extent, scale, bound, pieces=(), kind=jnp.bfloat16):
    level = shard_levels(own_key, extent, pieces, -0.22, 0.18) if pieces else 1.0
    entries = jax.random.normal(own_key, extent, jnp.float32) * scale * level
    return jnp.minimum(jnp.maximum(entries, -bound), bound).astype(kind)


def noise_with(stream_key, extent, spread, most, pieces, heavy, held_as=jnp.bfloat16):
    values = spread * jax.random.normal(stream_key, extent, jnp.float32)
    if pieces:
        values = values * shard_levels(stream_key, extent, pieces, -0.22, 0.18)
    return jnp.clip(with_spikes(values, jax.random.fold_in(stream_key, 3), *heavy), -most, most).astype(held_as)


def setup_inputs(seed: int = 0) -> dict:
    splits = jax.random.split(jax.random.key(seed), 13)
    return {
        "ptdf": noise_with(splits[0], (LINES, NODES), NODES ** -0.5, 0.0625, ((0, 4), (1, 16)), (1, 0, 16, 2.0)),
        "units_out": jnp.clip(1.5 * jax.random.uniform(splits[1], (HOURS, SCEN, UNITS), jnp.float32) ** shard_levels(splits[1], (HOURS, SCEN, UNITS), ((0, 2), (2, 16)), -0.2, 0.2), 0.0, 1.5),
        "load": noise(splits[2], (HOURS, SCEN, NODES), 1.0, 6.0, ((0, 2), (2, 16)), jnp.float32),
        "unit_node": draw_unit_node(jax.random.fold_in(splits[12], 71), 0),
        "commit_index": set_ends(jax.random.randint(splits[4], (HOURS, UNITS), 0, LEVELS), jax.random.fold_in(splits[4], 1), 0, LEVELS - 1).astype(jnp.int32),
        "relax_levels": jnp.clip(jax.random.uniform(splits[5], (LEVELS,), jnp.float32, 0.25, 1.0), 0.25, 1.0),
        "line_active": set_ends((jax.random.randint(splits[6], (HOURS, LINES), 0, 2) < 1).astype(jnp.int32), jax.random.fold_in(splits[6], 1), 0, 1),
        "line_limit": jnp.clip(0.3 + 1.2 * jax.random.uniform(splits[7], (LINES,), jnp.float32) ** shard_levels(splits[7], (LINES,), ((0, 4),), -0.2, 0.2), 0.3, 1.5),
        "line_weight": jnp.clip(jnp.exp(math.log(3.0) - 2.3025851 * jax.random.uniform(splits[8], (LINES,), jnp.float32) ** shard_levels(splits[8], (LINES,), ((0, 4),), -0.2, 0.2)), 0.3, 3.0),
        "ramp_active": set_ends((jax.random.randint(splits[9], (HOURS, UNITS), 0, 3) < 2).astype(jnp.int32), jax.random.fold_in(splits[9], 1), 0, 1),
        "ramp_limit": jnp.clip(0.05 + 0.35 * jax.random.uniform(splits[10], (UNITS,), jnp.float32) ** shard_levels(splits[10], (UNITS,), ((0, 16),), -0.2, 0.2), 0.05, 0.4),
        "ramp_weight": jnp.clip(jnp.exp(math.log(5.0) - 2.3025851 * jax.random.uniform(splits[11], (UNITS,), jnp.float32) ** shard_levels(splits[11], (UNITS,), ((0, 16),), -0.2, 0.2)), 0.5, 5.0),
    }


def hinge_grad(values, limits):
    return jax.nn.relu(values - limits) - jax.nn.relu(-values - limits)

def reference(ptdf, units_out, load, unit_node, commit_index, relax_levels, line_active, line_limit, line_weight, ramp_active, ramp_limit, ramp_weight):
    hours, scenarios, units = units_out.shape
    nodes = load.shape[2]
    level_ids = jnp.arange(relax_levels.shape[0], dtype=jnp.int32)
    unit_level = lax.optimization_barrier(jnp.sum(jnp.where(commit_index[:, :, None] == level_ids, relax_levels, jnp.float32(0.0)), axis=-1))
    generation = unit_level[:, None, :] * units_out
    placed = jnp.zeros((hours, scenarios, nodes), jnp.float32).at[:, :, unit_node].add(generation)
    injection = (placed - load).reshape(hours * scenarios, nodes).astype(jnp.bfloat16)
    flows = jnp.dot(ptdf, injection.T, preferred_element_type=jnp.float32)
    active = jnp.repeat(line_active.T, scenarios, axis=1).astype(jnp.float32)
    weights = 2.0 * line_weight[:, None] * active
    flow_grad = (weights * hinge_grad(flows, line_limit[:, None])).astype(jnp.bfloat16)
    node_grad = jnp.dot(flow_grad.T, ptdf, preferred_element_type=jnp.float32).reshape(hours, scenarios, nodes)
    unit_grad = node_grad[:, :, unit_node]
    ramp_step = generation[1:] - generation[:-1]
    ramp_mask = ramp_active[1:, None, :].astype(jnp.float32)
    inner = 2.0 * ramp_weight * ramp_mask * hinge_grad(ramp_step, ramp_limit)
    edge = jnp.zeros((1, scenarios, units), jnp.float32)
    ramp_dual = jnp.concatenate([edge, inner, edge], axis=0)
    return unit_level[:, None, :] * (unit_grad + ramp_dual[:-1] - ramp_dual[1:])
```

```python
import functools

import jax
import jax.numpy as jnp
from jax import lax
from jax.experimental import pallas as pl
from jax.experimental.pallas import tpu as pltpu
from jax.sharding import PartitionSpec as P

MESH = pl.DeviceIdType.MESH
F32 = jnp.float32
BF16 = jnp.bfloat16

CHUNKS = 6
QUARTER = 1280
HALF = 640
S1A, S1B, S2A, S2B, AGY, SUMZ, SUMX, AGZ = range(8)
KINDS = 8


def hinge_grad(values, limits):
    return jnp.maximum(values - limits, 0.0) - jnp.maximum(-values - limits, 0.0)


def kernel(
    ptdf_hbm, inj, node, act, lim, out,
    p, part_a, part_b, land_a, land_b, sum_a, sum_b, land2_a, land2_b, fg, u,
    land_z, sum_z, land_x, ob, onehot, g_send, g, p_sem, ssem, rsem, gs_sem, gr_sem, cs_sem, cr_sem,
):
    chunk = part_a.shape[2]
    sub = chunk // 4
    lines = ptdf_hbm.shape[0] // 4
    units = node.shape[1]
    hour = lax.axis_index("hour")
    bus = lax.axis_index("bus")
    z = lax.axis_index("line")
    x = bus // 4
    y = bus % 4

    def at(pos, j):
        return lax.rem(pos + (1, 3, 2)[j], 4)

    def dev_x(j):
        return (hour, at(x, j) * 4 + y, z)

    def dev_y(j):
        return (hour, x * 4 + at(y, j), z)

    def dev_z(j):
        return (hour, bus, at(z, j))

    sibling = (1 - hour, bus, z)

    def rows(pos):
        return pl.ds(pl.multiple_of(pos * sub, sub), sub)

    def lanes(pos):
        return pl.ds(pl.multiple_of(pos * units, units), units)

    def copy(kind, j, c):
        if kind == S1A:
            src, dst, dev = part_a.at[c, at(x, j)], land_a.at[c, j], dev_x(j)
        elif kind == S1B:
            src, dst, dev = part_b.at[c, :, rows(at(y, j))], land_b.at[c, j], dev_y(j)
        elif kind == S2A:
            src, dst, dev = sum_a.at[c, rows(at(y, j))], land2_a.at[c, j], dev_y(j)
        elif kind == S2B:
            src, dst, dev = sum_b.at[c, at(x, j)], land2_b.at[c, j], dev_x(j)
        elif kind == AGY:
            src, dst, dev = fg.at[c, rows(y)], fg.at[c, rows(y)], dev_y(j)
        elif kind == SUMZ:
            src, dst, dev = u.at[c, rows(at(z, j))], land_z.at[c, j], dev_z(j)
        elif kind == SUMX:
            src, dst, dev = sum_z.at[c, :, lanes(at(x, j))], land_x.at[c, j], dev_x(j)
        else:
            src, dst, dev = ob.at[c, rows(z)], ob.at[c, rows(z)], dev_z(j)
        return pltpu.make_async_remote_copy(
            src_ref=src, dst_ref=dst, send_sem=ssem.at[kind, j, c], recv_sem=rsem.at[kind, j, c],
            device_id=dev, device_id_type=MESH,
        )

    def send(kind, c):
        for j in (2, 0, 1):
            copy(kind, j, c).start()

    def receive(kind, c):
        for j in range(3):
            copy(kind, j, c).wait_recv()

    def load(q):
        return pltpu.make_async_copy(
            ptdf_hbm.at[pl.ds(pl.multiple_of(q * lines, 16), lines)],
            p.at[q, pl.ds(0, lines)], p_sem.at[q],
        )

    def g_rows(h):
        return pl.ds(pl.multiple_of(h * HALF, HALF), HALF)

    def g_copy(j):
        return pltpu.make_async_remote_copy(
            src_ref=g_send.at[j], dst_ref=g.at[x, g_rows(hour)], send_sem=gs_sem.at[j],
            recv_sem=gr_sem.at[j], device_id=dev_x(j), device_id_type=MESH,
        )

    def g_share(j):
        source = at(x, (1, 0, 2)[j])
        return pltpu.make_async_remote_copy(
            src_ref=g.at[source, g_rows(hour)], dst_ref=g.at[source, g_rows(hour)],
            send_sem=cs_sem.at[j], recv_sem=cr_sem.at[j], device_id=sibling, device_id_type=MESH,
        )

    def flows(c):
        columns = inj[pl.ds(pl.multiple_of(c * chunk, chunk), chunk), :]
        for k in range(4):
            q = lax.rem(x + 1 + k, 4)
            for half, part in ((0, part_a), (1, part_b)):
                part[c, q] = lax.dot_general(
                    columns, p[q, half * HALF : (half + 1) * HALF, :], (((1,), (1,)), ((), ())),
                    preferred_element_type=F32,
                ).astype(BF16)
        send(S1A, c)
        send(S1B, c)

    def step1(c):
        receive(S1A, c)
        total = part_a[c, x].astype(F32)
        for j in range(3):
            total = total + land_a[c, j].astype(F32)
        sum_a[c] = total.astype(BF16)
        send(S2A, c)
        receive(S1B, c)
        total = part_b[c, :, rows(y), :].astype(F32)
        for j in range(3):
            total = total + land_b[c, j].astype(F32)
        sum_b[c] = total.astype(BF16)
        send(S2B, c)

    def step2(c):
        receive(S2A, c)
        total = part_a[c, x, rows(y), :].astype(F32)
        for j in range(3):
            total = total + land_a[c, j, rows(y), :].astype(F32)
        for j in range(3):
            total = total + land2_a[c, j].astype(F32)
        fg[c, rows(y), 0:HALF] = (act[c, :, 0:HALF] * hinge_grad(total, lim[:, 0:HALF])).astype(BF16)
        receive(S2B, c)
        total = part_b[c, x, rows(y), :].astype(F32)
        for j in range(3):
            total = total + land_b[c, j, x].astype(F32)
        for j in range(3):
            total = total + land2_b[c, j].astype(F32)
        fg[c, rows(y), HALF:QUARTER] = (
            act[c, :, HALF:QUARTER] * hinge_grad(total, lim[:, HALF:QUARTER])
        ).astype(BF16)
        send(AGY, c)

    def step3(c):
        receive(AGY, c)
        for k in range(4):
            u[c, :, k * units : (k + 1) * units] = jnp.dot(
                fg[c], g[k], preferred_element_type=F32
            )
        send(SUMZ, c)

    def step4(c):
        receive(SUMZ, c)
        total = u[c, rows(z), :]
        for j in range(3):
            total = total + land_z[c, j]
        sum_z[c] = total
        send(SUMX, c)

    def step5(c):
        receive(SUMX, c)
        total = sum_z[c, :, lanes(x)]
        for j in range(3):
            total = total + land_x[c, j]
        ob[c, rows(z), :] = total
        send(AGZ, c)

    def step6(c):
        receive(AGZ, c)
        out[pl.ds(pl.multiple_of(c * chunk, chunk), chunk), :] = ob[c]
        for kind in range(KINDS):
            for j in range(3):
                copy(kind, j, c).wait_send()

    for q in range(4):
        load(q).start()
    barrier = pltpu.get_barrier_semaphore()
    for j in range(3):
        for dev in (dev_x(j), dev_y(j), dev_z(j)):
            pl.semaphore_signal(barrier, inc=1, device_id=dev, device_id_type=MESH)
    pl.semaphore_signal(barrier, inc=1, device_id=sibling, device_id_type=MESH)
    p[:, lines:QUARTER, :] = jnp.zeros((4, QUARTER - lines, p.shape[2]), BF16)
    onehot[...] = (
        lax.broadcasted_iota(jnp.int32, onehot.shape, 0) == node[...]
    ).astype(F32).astype(BF16)
    pl.semaphore_wait(barrier, 10)
    for q in range(4):
        load(q).wait()
    flows(0)
    for j in range(3):
        g_send[j] = jnp.dot(
            p[at(x, j), g_rows(hour), :], onehot[...], preferred_element_type=F32
        ).astype(BF16)
        g_copy(j).start()
    g[x] = jnp.dot(p[x], onehot[...], preferred_element_type=F32).astype(BF16)

    def body(i, carry):
        @pl.when(i >= 6)
        def _():
            step6(i - 6)

        @pl.when((i >= 5) & (i < CHUNKS + 5))
        def _():
            step5(i - 5)

        @pl.when((i >= 4) & (i < CHUNKS + 4))
        def _():
            step4(i - 4)

        @pl.when(i == 3)
        def _():
            for j in range(3):
                g_share(j).wait_recv()

        @pl.when((i >= 3) & (i < CHUNKS + 3))
        def _():
            step3(i - 3)

        @pl.when((i >= 2) & (i < CHUNKS + 2))
        def _():
            step2(i - 2)

        @pl.when(i == 2)
        def _():
            for j in range(3):
                g_copy(j).wait_recv()
                g_share(j).start()

        @pl.when(i < CHUNKS + 1)
        def _():
            step1(i - 1)

        @pl.when(i < CHUNKS)
        def _():
            flows(i)

        return carry

    lax.fori_loop(1, CHUNKS + 6, body, 0)
    for j in range(3):
        g_copy(j).wait_send()
        g_share(j).wait_send()


def node_gradient(ptdf, inj, node, act, lim):
    columns, nodes = inj.shape
    units = node.shape[1]
    chunk = columns // CHUNKS
    sub = chunk // 4
    vmem = pl.BlockSpec(memory_space=pltpu.VMEM)
    dma = pltpu.SemaphoreType.DMA
    return pl.pallas_call(
        kernel,
        out_shape=jax.ShapeDtypeStruct((columns, units), F32),
        in_specs=[pl.BlockSpec(memory_space=pl.ANY), vmem, vmem, vmem, vmem],
        out_specs=vmem,
        scratch_shapes=[
            pltpu.VMEM((4, QUARTER, nodes), BF16),
            pltpu.VMEM((CHUNKS, 4, chunk, HALF), BF16),
            pltpu.VMEM((CHUNKS, 4, chunk, HALF), BF16),
            pltpu.VMEM((CHUNKS, 3, chunk, HALF), BF16),
            pltpu.VMEM((CHUNKS, 3, 4, sub, HALF), BF16),
            pltpu.VMEM((CHUNKS, chunk, HALF), BF16),
            pltpu.VMEM((CHUNKS, 4, sub, HALF), BF16),
            pltpu.VMEM((CHUNKS, 3, sub, HALF), BF16),
            pltpu.VMEM((CHUNKS, 3, sub, HALF), BF16),
            pltpu.VMEM((CHUNKS, chunk, QUARTER), BF16),
            pltpu.VMEM((CHUNKS, chunk, 4 * units), F32),
            pltpu.VMEM((CHUNKS, 3, sub, 4 * units), F32),
            pltpu.VMEM((CHUNKS, sub, 4 * units), F32),
            pltpu.VMEM((CHUNKS, 3, sub, units), F32),
            pltpu.VMEM((CHUNKS, chunk, units), F32),
            pltpu.VMEM((nodes, units), BF16),
            pltpu.VMEM((3, HALF, units), BF16),
            pltpu.VMEM((4, QUARTER, units), BF16),
            dma((4,)),
            dma((KINDS, 3, CHUNKS)),
            dma((KINDS, 3, CHUNKS)),
            dma((3,)),
            dma((3,)),
            dma((3,)),
            dma((3,)),
        ],
        compiler_params=pltpu.CompilerParams(
            collective_id=0, has_side_effects=True, vmem_limit_bytes=60 << 20
        ),
    )(ptdf, inj, node, act, lim)


def body(
    ptdf, units_out, load, unit_node, commit_index, relax_levels,
    line_active, line_limit, line_weight, ramp_active, ramp_limit, ramp_weight,
):
    hours_dev, scenarios, units_dev = units_out.shape
    lines_dev, nodes_dev = ptdf.shape
    columns = hours_dev * scenarios
    bus_pos = lax.axis_index("bus")
    hour_pos = lax.axis_index("hour")
    x, y = bus_pos // 4, bus_pos % 4
    level_ids = jnp.arange(relax_levels.shape[0], dtype=jnp.int32)
    unit_level = jnp.sum(
        jnp.where(commit_index[:, :, None] == level_ids, relax_levels, jnp.float32(0.0)), axis=-1
    )
    generation = unit_level[:, None, :] * units_out
    local_node = unit_node - bus_pos * nodes_dev
    onehot = (local_node[:, None] == jnp.arange(nodes_dev, dtype=jnp.int32)).astype(F32)
    placed = jnp.dot(
        generation.reshape(columns, units_dev), onehot, precision=lax.Precision.HIGHEST
    )
    injection = (placed - load.reshape(columns, nodes_dev)).astype(BF16)

    lines = lines_dev // 4
    sub_hours = hours_dev // CHUNKS // 4

    def own_lines(array):
        block = lax.dynamic_slice_in_dim(array, x * lines, lines, -1)
        pad = [(0, 0)] * (block.ndim - 1) + [(0, QUARTER - lines)]
        return jnp.pad(block, pad)

    active = lax.dynamic_slice_in_dim(
        line_active.reshape(CHUNKS, 4, sub_hours, lines_dev), y, 1, 1
    )[:, 0]
    active = own_lines(active).astype(F32)
    weights = own_lines(2.0 * line_weight) * active
    act = jnp.repeat(weights, scenarios, axis=1)
    lim = own_lines(line_limit)[None, :]
    unit_grad = node_gradient(ptdf, injection, local_node[None, :], act, lim).reshape(
        hours_dev, scenarios, units_dev
    )

    hours_all = hours_dev * lax.axis_size("hour")
    low = lax.ppermute(generation[-1:], "hour", [(0, 1)])
    high = lax.ppermute(generation[:1], "hour", [(1, 0)])
    padded = jnp.concatenate([low, generation, high], axis=0)
    ramp_step = padded[1:] - padded[:-1]
    hour_ids = hour_pos * hours_dev + jnp.arange(hours_dev + 1, dtype=jnp.int32)
    inside = ((hour_ids >= 1) & (hour_ids <= hours_all - 1)).astype(F32)
    extended = jnp.concatenate([ramp_active, jnp.zeros((1, units_dev), jnp.int32)], axis=0)
    ramp_rows = lax.dynamic_slice_in_dim(
        extended, hour_pos * hours_dev, hours_dev + 1, 0
    ).astype(F32)
    ramp_mask = (ramp_rows * inside[:, None])[:, None, :]
    ramp_dual = 2.0 * ramp_weight * ramp_mask * hinge_grad(ramp_step, ramp_limit)
    return unit_level[:, None, :] * (unit_grad + ramp_dual[:-1] - ramp_dual[1:])


def solution(mesh):
    return jax.shard_map(
        body,
        mesh=mesh,
        in_specs=(
            P("line", "bus"),
            P("hour", None, "bus"),
            P("hour", None, "bus"),
            P("bus"),
            P("hour", "bus"),
            P(),
            P("hour", "line"),
            P("line"),
            P("line"),
            P(None, "bus"),
            P("bus"),
            P("bus"),
        ),
        out_specs=P("hour", None, "bus"),
        check_vma=False,
    )
```

```python
import jax
import jax.numpy as jnp
from jax import lax
from jax.experimental import pallas as pl
from jax.experimental.pallas import tpu as pltpu
from jax.sharding import PartitionSpec as P

MESH = pl.DeviceIdType.MESH
F32 = jnp.float32
BF16 = jnp.bfloat16

CHUNKS = 6
BLOCK = 128
HALF = 640
QUARTER = 2 * HALF
SCEN = 8
OA, DA, RA, OB, DB, RB, S2A, S2B, AGY, SUMZ, SUMX, AGZ = range(12)
KINDS = 12
WIDE = (S2A, S2B, AGY, SUMZ, SUMX, AGZ)


def hinge_grad(values, limits):
    return jnp.maximum(values - limits, 0.0) - jnp.maximum(-values - limits, 0.0)


def kernel(
    levels, ptdf_hbm, load_hbm, units_hbm, commit_hbm, active_hbm, ramp_hbm,
    node, limit, weight, ramp_limit, ramp_weight, out,
    p, load, units, commit, active, ramp, lev, gx, rw, lim, wgt, inj,
    part_a, part_b, own_a, relay_a, relay_b, land_a, land_b, sum_a, sum_b, land2_a, land2_b,
    fg, u, land_z, sum_z, land_x, ob, onehot, g_send, g,
    p_sem, in_sem, ssem, rsem, gs_sem, gr_sem, cs_sem, cr_sem, halo_sem,
):
    columns, nodes = load.shape
    hours = columns // SCEN
    lines = ptdf_hbm.shape[0]
    n_units = node.shape[1]
    chunk = columns // CHUNKS
    sub = chunk // 4
    hour = lax.axis_index("hour")
    bus = lax.axis_index("bus")
    z = lax.axis_index("line")
    x = bus // 4
    y = bus % 4
    sibling = (1 - hour, bus, z)

    def at(pos, j):
        return lax.rem(pos + (1, 3, 2)[j], 4)

    def dev_x(j):
        return (hour, at(x, j) * 4 + y, z)

    def dev_y(j):
        return (hour, x * 4 + at(y, j), z)

    def dev_z(j):
        return (hour, bus, at(z, j))

    def span(start, size):
        return pl.ds(pl.multiple_of(start, size), size)

    def rows(c):
        return span(c * chunk, chunk)

    def rows_of(c, pos):
        return span(c * chunk + pos * sub, sub)

    def half_rows(c, h):
        return span(c * chunk + h * (chunk // 2), chunk // 2)

    def quarter(q):
        return span(q * QUARTER, QUARTER)

    def copy(kind, j, c):
        own = span(c * sub, sub)
        if kind == OA:
            src = part_a.at[at(x, 2), half_rows(c, j)]
            dst, dev = relay_a.at[j, span(c * (chunk // 2), chunk // 2)], dev_x(j)
        elif kind == DA:
            src = part_a.at[at(x, j), half_rows(c, 1 - j)]
            dst, dev = land_a.at[j, half_rows(c, 1 - j)], dev_x(j)
        elif kind == RA:
            src = part_a.at[at(x, j), half_rows(c, j)]
            dst, dev = land_a.at[j, half_rows(c, j)], dev_x(j)
        elif kind == OB:
            src = part_b.at[pl.ds(2 * j, 2), rows_of(c, at(y, 2))]
            dst, dev = relay_b.at[j, :, own], dev_y(j)
        elif kind == DB:
            src = part_b.at[pl.ds(2 - 2 * j, 2), rows_of(c, at(y, j))]
            dst, dev = land_b.at[j, pl.ds(2 - 2 * j, 2), own], dev_y(j)
        elif kind == RB:
            src = part_b.at[pl.ds(2 * j, 2), rows_of(c, at(y, j))]
            dst, dev = land_b.at[j, pl.ds(2 * j, 2), own], dev_y(j)
        elif kind == S2A:
            src, dst, dev = sum_a.at[rows_of(c, at(y, j))], land2_a.at[j, own], dev_y(j)
        elif kind == S2B:
            src, dst, dev = sum_b.at[at(x, j), own], land2_b.at[j, own], dev_x(j)
        elif kind == AGY:
            src, dst, dev = fg.at[rows_of(c, y)], fg.at[rows_of(c, y)], dev_y(j)
        elif kind == SUMZ:
            src, dst, dev = u.at[rows_of(c, at(z, j))], land_z.at[j, own], dev_z(j)
        elif kind == SUMX:
            src = sum_z.at[own, span(at(x, j) * n_units, n_units)]
            dst, dev = land_x.at[j, own], dev_x(j)
        else:
            src, dst, dev = ob.at[rows_of(c, z)], ob.at[rows_of(c, z)], dev_z(j)
        return pltpu.make_async_remote_copy(
            src_ref=src, dst_ref=dst, send_sem=ssem.at[kind, j, c], recv_sem=rsem.at[kind, j, c],
            device_id=dev, device_id_type=MESH,
        )

    def ways(kind):
        return (2, 0, 1) if kind in WIDE else (0, 1)

    def send(kind, c):
        for j in ways(kind):
            copy(kind, j, c).start()

    def receive(kind, c):
        for j in ways(kind):
            copy(kind, j, c).wait_recv()

    def fetch(q, do):
        last = lines - 3 * QUARTER

        @pl.when(q < 3)
        def _():
            do(pltpu.make_async_copy(ptdf_hbm.at[quarter(q)], p.at[quarter(q)], p_sem.at[q]))

        @pl.when(q == 3)
        def _():
            part = pl.ds(3 * QUARTER, last)
            do(pltpu.make_async_copy(ptdf_hbm.at[part], p.at[part], p_sem.at[3]))

    def g_rows(h):
        return span(h * HALF, HALF)

    def g_copy(j):
        return pltpu.make_async_remote_copy(
            src_ref=g_send.at[j], dst_ref=g.at[x, g_rows(hour)], send_sem=gs_sem.at[j],
            recv_sem=gr_sem.at[j], device_id=dev_x(j), device_id_type=MESH,
        )

    def g_share(j):
        source = at(x, (1, 0, 2)[j])
        return pltpu.make_async_remote_copy(
            src_ref=g.at[source, g_rows(hour)], dst_ref=g.at[source, g_rows(hour)],
            send_sem=cs_sem.at[j], recv_sem=cr_sem.at[j], device_id=sibling, device_id_type=MESH,
        )

    def halo():
        return pltpu.make_async_remote_copy(
            src_ref=gx.at[hours - (hours - 1) * hour], dst_ref=gx.at[(hours + 1) * hour],
            send_sem=halo_sem.at[0], recv_sem=halo_sem.at[1], device_id=sibling, device_id_type=MESH,
        )

    def injection(b):
        per = BLOCK // SCEN
        rest = gx[pl.ds(1 + b * per, per)].reshape(BLOCK, n_units)
        total = -load[span(b * BLOCK, BLOCK), :]
        placed = None
        for _ in range(3):
            head = rest.astype(BF16)
            rest = rest - head.astype(F32)
            term = lax.dot_general(
                head, onehot[...], (((1,), (1,)), ((), ())), preferred_element_type=F32
            )
            placed = term if placed is None else placed + term
        inj[...] = (placed + total).astype(BF16)

    def flows(b, first=False):
        injection(b)
        where = span(b * BLOCK, BLOCK)
        for k in (2, 0, 1, 3):
            q = lax.rem(x + (1, 3, 2, 0)[k], 4)
            if first:
                fetch(q, lambda dma: dma.wait())
            for half in range(2):
                flow = lax.dot_general(
                    inj[...], p[span(q * QUARTER + half * HALF, HALF), :],
                    (((1,), (1,)), ((), ())), preferred_element_type=F32,
                )
                if half == 1:
                    part_b[q, where] = flow.astype(BF16)
                elif k == 3:
                    own_a[where] = flow
                else:
                    part_a[q, where] = flow.astype(BF16)

    def start(c):
        for kind in (OA, OB, DA, DB):
            send(kind, c)

    def relay(c):
        own = span(c * sub, sub)
        for j in range(2):
            copy(OA, j, c).wait_recv()
            q, where = at(x, j), half_rows(c, j)
            there = relay_a[j, span(c * (chunk // 2), chunk // 2), :]
            part_a[q, where, :] = (part_a[q, where, :].astype(F32) + there.astype(F32)).astype(BF16)
            copy(RA, j, c).start()
            copy(OB, j, c).wait_recv()
            where = rows_of(c, at(y, j))
            mine = part_b[2 * j : 2 * j + 2, where, :]
            part_b[2 * j : 2 * j + 2, where, :] = (
                mine.astype(F32) + relay_b[j, :, own, :].astype(F32)
            ).astype(BF16)
            copy(RB, j, c).start()

    def total_a(where):
        return own_a[where, :] + land_a[0, where, :].astype(F32) + land_a[1, where, :].astype(F32)

    def step1(c):
        own = span(c * sub, sub)
        receive(DA, c)
        receive(RA, c)
        sum_a[rows(c), :] = total_a(rows(c)).astype(BF16)
        send(S2A, c)
        receive(DB, c)
        receive(RB, c)
        total = part_b[:, rows_of(c, y), :].astype(F32)
        for j in range(2):
            total = total + land_b[j, :, own, :].astype(F32)
        sum_b[:, own, :] = total.astype(BF16)
        send(S2B, c)

    def step2(c):
        own = span(c * sub, sub)
        per = sub // SCEN
        line = quarter(x)
        mask = jnp.concatenate(
            [
                jnp.broadcast_to(
                    active[pl.ds(c * (4 * per) + y * per + k, 1), line].astype(F32), (SCEN, QUARTER)
                )
                for k in range(per)
            ],
            axis=0,
        )
        scale = 2.0 * wgt[:, line] * mask
        bound = lim[:, line]
        receive(S2A, c)
        total = total_a(rows_of(c, y))
        for j in range(3):
            total = total + land2_a[j, own, :].astype(F32)
        fg[rows_of(c, y), 0:HALF] = (
            scale[:, 0:HALF] * hinge_grad(total, bound[:, 0:HALF])
        ).astype(BF16)
        receive(S2B, c)
        total = part_b[x, rows_of(c, y), :].astype(F32)
        for j in range(2):
            total = total + land_b[j, x, own, :].astype(F32)
        for j in range(3):
            total = total + land2_b[j, own, :].astype(F32)
        fg[rows_of(c, y), HALF:QUARTER] = (
            scale[:, HALF:QUARTER] * hinge_grad(total, bound[:, HALF:QUARTER])
        ).astype(BF16)
        send(AGY, c)

    def step3(c):
        receive(AGY, c)
        for k in range(4):
            u[rows(c), k * n_units : (k + 1) * n_units] = jnp.dot(
                fg[rows(c), :], g[k], preferred_element_type=F32
            )
        send(SUMZ, c)

    def step4(c):
        receive(SUMZ, c)
        own = span(c * sub, sub)
        total = u[rows_of(c, z), :]
        for j in range(3):
            total = total + land_z[j, own, :]
        sum_z[own, :] = total
        send(SUMX, c)

    def step5(c):
        receive(SUMX, c)
        own = span(c * sub, sub)
        total = sum_z[own, span(x * n_units, n_units)]
        for j in range(3):
            total = total + land_x[j, own, :]
        ob[rows_of(c, z), :] = total
        send(AGZ, c)

    def step6(c):
        per = chunk // SCEN
        grid = (per, SCEN, n_units)
        step = gx[pl.ds(c * per + 1, per + 1)] - gx[pl.ds(c * per, per + 1)]
        dual = rw[pl.ds(c * per, per + 1)] * hinge_grad(step, ramp_limit[...][None])
        receive(AGZ, c)
        grad = ob[rows(c), :].reshape(grid) + dual[:-1] - dual[1:]
        out[rows(c), :] = (lev[pl.ds(c * per, per)] * grad).reshape(chunk, n_units)
        for kind in range(KINDS):
            for j in ways(kind):
                copy(kind, j, c).wait_send()

    locals_in = [
        pltpu.make_async_copy(src, dst, in_sem.at[n])
        for n, (src, dst) in enumerate(
            [
                (commit_hbm, commit),
                (units_hbm, units),
                (load_hbm, load),
                (active_hbm, active.at[:, pl.ds(0, lines)]),
                (ramp_hbm, ramp),
            ]
        )
    ]
    for dma in locals_in[:3]:
        dma.start()
    for k in (2, 0, 1, 3):
        fetch(lax.rem(x + (1, 3, 2, 0)[k], 4), lambda dma: dma.start())
    for dma in locals_in[3:]:
        dma.start()
    barrier = pltpu.get_barrier_semaphore()
    for j in range(3):
        for dev in (dev_x(j), dev_y(j), dev_z(j)):
            pl.semaphore_signal(barrier, inc=1, device_id=dev, device_id_type=MESH)
    pl.semaphore_signal(barrier, inc=1, device_id=sibling, device_id_type=MESH)

    fill = 4 * QUARTER - lines
    p[lines:, :] = jnp.zeros((fill, nodes), BF16)
    active[:, lines:] = jnp.zeros((hours, fill), jnp.int32)
    lim[:, lines:] = jnp.zeros((1, fill), F32)
    wgt[:, lines:] = jnp.zeros((1, fill), F32)
    lim[:, :lines] = limit[...]
    wgt[:, :lines] = weight[...]
    onehot[...] = (
        lax.broadcasted_iota(jnp.int32, onehot.shape, 0) == node[...] - bus * nodes
    ).astype(F32).astype(BF16)
    gx[(hours + 1) * hour] = jnp.zeros((SCEN, n_units), F32)
    locals_in[0].wait()
    locals_in[1].wait()

    def generate(k, carry):
        row = commit[pl.ds(k, 1), :]
        value = jnp.zeros((1, n_units), F32)
        for n in range(levels.shape[0]):
            value = value + jnp.where(row == n, levels[n], 0.0)
        value = jnp.broadcast_to(value, (SCEN, n_units))
        lev[k] = value
        gx[k + 1] = value * units[k]
        return carry

    lax.fori_loop(0, hours, generate, 0)
    locals_in[2].wait()
    flows(0, first=True)
    pl.semaphore_wait(barrier, 10)
    start(0)
    halo().start()
    for j in range(3):
        g_send[j] = jnp.dot(
            p[span(at(x, j) * QUARTER + hour * HALF, HALF), :], onehot[...],
            preferred_element_type=F32,
        ).astype(BF16)
        g_copy(j).start()
    g[x] = jnp.dot(p[quarter(x), :], onehot[...], preferred_element_type=F32).astype(BF16)
    locals_in[3].wait()
    locals_in[4].wait()

    def ramps(k, carry):
        index = lax.rem(hour * hours + k, 2 * hours)
        inner = (index != 0).astype(F32)
        row = 2.0 * ramp_weight[...] * (ramp[pl.ds(index, 1), :].astype(F32) * inner)
        rw[k] = jnp.broadcast_to(row, (SCEN, n_units))
        return carry

    lax.fori_loop(0, hours + 1, ramps, 0)
    halo().wait()

    stages = [(flows, 0), (step6, 7), (step5, 6), (step4, 5), (step3, 4), (step2, 3), (step1, 2), (relay, 1)]
    per = BLOCK // chunk

    def body(i, carry):
        @pl.when(i < CHUNKS)
        def _():
            if per == 1:
                flows(i)
            else:
                @pl.when(lax.rem(i, per) == 0)
                def _():
                    flows(i // per)
            start(i)

        for stage, lag in stages[1:]:
            if stage is step3:
                @pl.when(i == lag)
                def _():
                    for j in range(3):
                        g_share(j).wait_recv()

            @pl.when((i >= lag) & (i < CHUNKS + lag))
            def _():
                stage(i - lag)

            if stage is step2:
                @pl.when(i == lag)
                def _():
                    for j in range(3):
                        g_copy(j).wait_recv()
                        g_share(j).start()

        return carry

    lax.fori_loop(1, CHUNKS + 7, body, 0)
    for j in range(3):
        g_copy(j).wait_send()
        g_share(j).wait_send()


def body(
    ptdf, units_out, load, unit_node, commit_index, relax_levels,
    line_active, line_limit, line_weight, ramp_active, ramp_limit, ramp_weight,
):
    hours, scen, units = units_out.shape
    lines, nodes = ptdf.shape
    columns = hours * scen
    vmem = pl.BlockSpec(memory_space=pltpu.VMEM)
    smem = pl.BlockSpec(memory_space=pltpu.SMEM)
    anywhere = pl.BlockSpec(memory_space=pl.ANY)
    dma = pltpu.SemaphoreType.DMA
    all_lines = 4 * QUARTER
    own = columns // 4
    grad = pl.pallas_call(
        kernel,
        out_shape=jax.ShapeDtypeStruct((columns, units), F32),
        in_specs=[smem] + [anywhere] * 6 + [vmem] * 5,
        out_specs=vmem,
        scratch_shapes=[
            pltpu.VMEM((all_lines, nodes), BF16),
            pltpu.VMEM((columns, nodes), F32),
            pltpu.VMEM((hours, scen, units), F32),
            pltpu.VMEM((hours, units), jnp.int32),
            pltpu.VMEM((hours, all_lines), jnp.int32),
            pltpu.VMEM((2 * hours, units), jnp.int32),
            pltpu.VMEM((hours, scen, units), F32),
            pltpu.VMEM((hours + 2, scen, units), F32),
            pltpu.VMEM((hours + 1, scen, units), F32),
            pltpu.VMEM((1, all_lines), F32),
            pltpu.VMEM((1, all_lines), F32),
            pltpu.VMEM((BLOCK, nodes), BF16),
            pltpu.VMEM((4, columns, HALF), BF16),
            pltpu.VMEM((4, columns, HALF), BF16),
            pltpu.VMEM((columns, HALF), F32),
            pltpu.VMEM((2, columns // 2, HALF), BF16),
            pltpu.VMEM((2, 2, own, HALF), BF16),
            pltpu.VMEM((2, columns, HALF), BF16),
            pltpu.VMEM((2, 4, own, HALF), BF16),
            pltpu.VMEM((columns, HALF), BF16),
            pltpu.VMEM((4, own, HALF), BF16),
            pltpu.VMEM((3, own, HALF), BF16),
            pltpu.VMEM((3, own, HALF), BF16),
            pltpu.VMEM((columns, QUARTER), BF16),
            pltpu.VMEM((columns, 4 * units), F32),
            pltpu.VMEM((3, own, 4 * units), F32),
            pltpu.VMEM((own, 4 * units), F32),
            pltpu.VMEM((3, own, units), F32),
            pltpu.VMEM((columns, units), F32),
            pltpu.VMEM((nodes, units), BF16),
            pltpu.VMEM((3, HALF, units), BF16),
            pltpu.VMEM((4, QUARTER, units), BF16),
            dma((4,)),
            dma((5,)),
            dma((KINDS, 3, CHUNKS)),
            dma((KINDS, 3, CHUNKS)),
            dma((3,)),
            dma((3,)),
            dma((3,)),
            dma((3,)),
            dma((2,)),
        ],
        compiler_params=pltpu.CompilerParams(
            collective_id=0, has_side_effects=True, vmem_limit_bytes=62 << 20
        ),
    )(
        relax_levels, ptdf, load.reshape(columns, nodes), units_out, commit_index, line_active,
        ramp_active, unit_node[None, :], line_limit[None, :], line_weight[None, :],
        ramp_limit[None, :], ramp_weight[None, :],
    )
    return grad.reshape(hours, scen, units)


def solution(mesh):
    return jax.shard_map(
        body,
        mesh=mesh,
        in_specs=(
            P("line", "bus"),
            P("hour", None, "bus"),
            P("hour", None, "bus"),
            P("bus"),
            P("hour", "bus"),
            P(),
            P("hour", "line"),
            P("line"),
            P("line"),
            P(None, "bus"),
            P("bus"),
            P("bus"),
        ),
        out_specs=P("hour", None, "bus"),
        check_vma=False,
    )
```

```python
import jax
import jax.numpy as jnp
from jax import lax
from jax.experimental import pallas as pl
from jax.experimental.pallas import tpu as pltpu
from jax.sharding import PartitionSpec as P

MESH = pl.DeviceIdType.MESH
F32 = jnp.float32
BF16 = jnp.bfloat16

CHUNKS = 6
HALF = 640
QUARTER = 2 * HALF
SCEN = 8
OA, OB, TA, TB, S2A, S2B, AGY, SUMZ, SUMX, AGZ = range(10)
KINDS = 10
ORDER = (("F", 0), ("6", 20), ("1", 4), ("3", 8), ("5", 15), ("R", 2), ("4", 12), ("2", 5))


def hinge_grad(values, limits):
    return jnp.maximum(values - limits, 0.0) - jnp.maximum(-values - limits, 0.0)


def kernel(
    levels, ptdf_hbm, load_hbm, units_hbm, commit_hbm, active_hbm, ramp_hbm, limit_hbm, weight_hbm,
    node, ramp_limit, ramp_weight, out,
    p, load, units, commit, active, ramp, lev, gx, rw, lim, wgt, inj,
    part_a, part_b, own_a, relay_a, relay_b, land_a, land_b, sum_a, sum_b, land2_a, land2_b,
    fg, u, u_send, land_z, sum_z, land_x, ob, onehot, g_send, g,
    p_sem, in_sem, ssem, rsem, g_sem, halo_sem,
):
    columns, nodes = load.shape
    hours = columns // SCEN
    lines = ptdf_hbm.shape[0]
    n_units = node.shape[1]
    chunk = columns // CHUNKS
    sub = chunk // 4
    hour = lax.axis_index("hour")
    bus = lax.axis_index("bus")
    z = lax.axis_index("line")
    x = bus // 4
    y = bus % 4
    sibling = (1 - hour, bus, z)

    def at(pos, j):
        return lax.rem(pos + (1, 3, 2)[j], 4)

    def dev_x(j):
        return (hour, at(x, j) * 4 + y, z)

    def dev_y(j):
        return (hour, x * 4 + at(y, j), z)

    def dev_z(j):
        return (hour, bus, at(z, j))

    def span(start, size):
        return pl.ds(pl.multiple_of(start, size), size)

    def rows(c):
        return span(c * chunk, chunk)

    def own(c):
        return span(c * sub, sub)

    def rows_of(c, pos):
        return span(c * chunk + pos * sub, sub)

    def half_rows(c, h):
        return span(c * chunk + h * (chunk // 2), chunk // 2)

    def own_rows(c, times):
        return pl.ds(pl.multiple_of(c * chunk, chunk), times * sub)

    def over_rows(start, size, step, work):
        @pl.loop(0, size // step)
        def _(k):
            work(span(start + k * step, step))

    def quarter(q):
        return pl.ds(pl.multiple_of(q * QUARTER, QUARTER), QUARTER)

    def unit_lanes(pos):
        return pl.ds(pl.multiple_of(pos * n_units, n_units), n_units)

    def push(src, dst, send_sem, recv_sem, dev):
        pltpu.make_async_remote_copy(
            src_ref=src, dst_ref=dst, send_sem=send_sem, recv_sem=recv_sem,
            device_id=dev, device_id_type=MESH,
        ).start()

    def take(ref, sem):
        pltpu.make_async_copy(ref, ref, sem).wait()

    def receive(kind, c, ref):
        take(ref, rsem.at[kind, c])

    def fetch(q, do):
        last = lines - 3 * QUARTER

        @pl.when(q < 3)
        def _():
            do(pltpu.make_async_copy(ptdf_hbm.at[quarter(q)], p.at[quarter(q)], p_sem.at[q]))

        @pl.when(q == 3)
        def _():
            part = pl.ds(3 * QUARTER, last)
            do(pltpu.make_async_copy(ptdf_hbm.at[part], p.at[part], p_sem.at[3]))

    def injection(c):
        per = chunk // SCEN
        rest = gx[pl.ds(1 + c * per, per)].reshape(chunk, n_units)
        placed = None
        for _ in range(3):
            head = rest.astype(BF16)
            rest = rest - head.astype(F32)
            term = lax.dot_general(
                head, onehot[...], (((1,), (1,)), ((), ())), preferred_element_type=F32
            )
            placed = term if placed is None else placed + term
        inj[...] = (placed - load[rows(c), :]).astype(BF16)

    def product(q, half):
        where = pl.ds(pl.multiple_of(q * QUARTER + half * HALF, HALF), HALF)
        return lax.dot_general(
            inj[...], p[where, :], (((1,), (1,)), ((), ())), preferred_element_type=F32
        )

    def forward(c):
        injection(c)

        @pl.loop(0, 4)
        def _(k):
            q = lax.rem(x + 2 + k, 4)

            @pl.when(c == 0)
            def _():
                fetch(q, lambda dma: dma.wait())

            flow = product(q, 0)
            part_a[q, rows(c)] = flow.astype(BF16)

            @pl.when(k == 2)
            def _():
                own_a[rows(c)] = flow

            part_b[q, rows(c)] = product(q, 1).astype(BF16)

        @pl.when(c == 0)
        def _():
            pl.semaphore_wait(pltpu.get_barrier_semaphore(), 10)

        for j in range(2):
            push(part_a.at[at(x, 2), half_rows(c, j)], relay_a.at[half_rows(c, j)],
                 ssem.at[OA], rsem.at[OA, c], dev_x(j))
            pair = pl.ds(2 * j, 2)
            push(part_b.at[pair, rows_of(c, at(y, 2))], relay_b.at[pair, own(c)],
                 ssem.at[OB], rsem.at[OB, c], dev_y(j))
        for j in range(2):
            half = half_rows(c, 1 - j)
            push(part_a.at[at(x, j), half], land_a.at[j, half], ssem.at[OA], rsem.at[TA, c], dev_x(j))
            pair = pl.ds(2 - 2 * j, 2)
            push(part_b.at[pair, rows_of(c, at(y, j))], land_b.at[j, pair, own(c)],
                 ssem.at[OB], rsem.at[TB, c], dev_y(j))

    def relay(c):
        receive(OA, c, relay_a.at[rows(c)])
        for j in range(2):
            q = at(x, j)

            def add_a(where):
                part_a[q, where, :] = (
                    part_a[q, where, :].astype(F32) + relay_a[where, :].astype(F32)
                ).astype(BF16)

            over_rows(c * chunk + j * (chunk // 2), chunk // 2, 16, add_a)
            half = half_rows(c, j)
            push(part_a.at[q, half], land_a.at[j, half], ssem.at[OA], rsem.at[TA, c], dev_x(j))
        receive(OB, c, relay_b.at[:, own(c)])
        for j in range(2):
            where = rows_of(c, at(y, j))

            @pl.loop(2 * j, 2 * j + 2)
            def _(q):
                part_b[q, where, :] = (
                    part_b[q, where, :].astype(F32) + relay_b[q, own(c), :].astype(F32)
                ).astype(BF16)

            pair = pl.ds(2 * j, 2)
            push(part_b.at[pair, where], land_b.at[j, pair, own(c)],
                 ssem.at[OB], rsem.at[TB, c], dev_y(j))

    def total_a(where):
        return own_a[where, :] + land_a[0, where, :].astype(F32) + land_a[1, where, :].astype(F32)

    def total_b(c, q):
        total = part_b[q, rows_of(c, y), :].astype(F32)
        for j in range(2):
            total = total + land_b[j, q, own(c), :].astype(F32)
        return total

    def step1(c):
        receive(TA, c, land_a.at[:, rows(c)])

        def add_a(where):
            sum_a[where, :] = total_a(where).astype(BF16)

        over_rows(c * chunk, chunk, 16, add_a)
        for j in (2, 0, 1):
            push(sum_a.at[rows_of(c, at(y, j))], land2_a.at[j, own(c)],
                 ssem.at[S2A], rsem.at[S2A, c], dev_y(j))
        receive(TB, c, land_b.at[:, :, own(c)])

        @pl.loop(0, 4)
        def _(q):
            sum_b[q, own(c), :] = total_b(c, q).astype(BF16)

        for j in (2, 0, 1):
            push(sum_b.at[at(x, j), own(c)], land2_b.at[j, own(c)],
                 ssem.at[S2B], rsem.at[S2B, c], dev_x(j))

    def step2(c):
        per = sub // SCEN
        line = quarter(x)
        mask = jnp.concatenate(
            [
                jnp.broadcast_to(
                    active[pl.ds((c * 4 + y) * per + k, 1), line].astype(F32), (SCEN, QUARTER)
                )
                for k in range(per)
            ],
            axis=0,
        )
        scale = 2.0 * wgt[:, line] * mask
        bound = lim[:, line]
        where = rows_of(c, y)
        receive(S2A, c, land2_a.at[:, own(c)])
        total = total_a(where)
        for j in range(3):
            total = total + land2_a[j, own(c), :].astype(F32)
        fg[where, 0:HALF] = (scale[:, 0:HALF] * hinge_grad(total, bound[:, 0:HALF])).astype(BF16)
        receive(S2B, c, land2_b.at[:, own(c)])
        total = total_b(c, x)
        for j in range(3):
            total = total + land2_b[j, own(c), :].astype(F32)
        fg[where, HALF:QUARTER] = (
            scale[:, HALF:QUARTER] * hinge_grad(total, bound[:, HALF:QUARTER])
        ).astype(BF16)
        for j in (2, 0, 1):
            push(fg.at[where], fg.at[where], ssem.at[AGY], rsem.at[AGY, c], dev_y(j))

    def step3(c):
        @pl.when(c == 0)
        def _():
            take(g_send, g_sem.at[3])

        receive(AGY, c, fg.at[own_rows(c, 3)])

        @pl.loop(0, 4)
        def _(k):
            grad = jnp.dot(fg[rows(c), :], g[k], preferred_element_type=F32)
            u[rows(c), unit_lanes(k)] = grad
            u_send[rows(c), unit_lanes(k)] = grad.astype(BF16)

        for j in (2, 0, 1):
            push(u_send.at[rows_of(c, at(z, j))], land_z.at[j, own(c)],
                 ssem.at[SUMZ], rsem.at[SUMZ, c], dev_z(j))

    def step4(c):
        receive(SUMZ, c, land_z.at[:, own(c)])

        @pl.loop(0, 4)
        def _(k):
            total = u[rows_of(c, z), unit_lanes(k)]
            for j in range(3):
                total = total + land_z[j, own(c), unit_lanes(k)].astype(F32)
            sum_z[own(c), unit_lanes(k)] = total

        for j in (2, 0, 1):
            push(sum_z.at[own(c), unit_lanes(at(x, j))], land_x.at[j, own(c)],
                 ssem.at[SUMX], rsem.at[SUMX, c], dev_x(j))

    def step5(c):
        receive(SUMX, c, land_x.at[:, own(c)])
        total = sum_z[own(c), unit_lanes(x)]
        for j in range(3):
            total = total + land_x[j, own(c), :]
        where = rows_of(c, z)
        ob[where, :] = total
        for j in (2, 0, 1):
            push(ob.at[where], ob.at[where], ssem.at[AGZ], rsem.at[AGZ, c], dev_z(j))

    def step6(c):
        receive(AGZ, c, ob.at[own_rows(c, 3)])
        per = chunk // SCEN
        bound = ramp_limit[...][None]

        @pl.loop(0, per // 4)
        def _(k):
            h = c * per + k * 4
            step = gx[pl.ds(h + 1, 5)] - gx[pl.ds(h, 5)]
            dual = rw[pl.ds(h, 5)] * hinge_grad(step, bound)
            where = span(h * SCEN, 4 * SCEN)
            grad = ob[where, :].reshape(4, SCEN, n_units) + dual[:-1] - dual[1:]
            out[where, :] = (lev[pl.ds(h, 4)] * grad).reshape(4 * SCEN, n_units)

    def g_rows(h):
        return pl.ds(pl.multiple_of(h * HALF, HALF), HALF)

    def send_factor(j):
        where = pl.ds(pl.multiple_of(at(x, j) * QUARTER + hour * HALF, HALF), HALF)
        g_send[j] = jnp.dot(p[where, :], onehot[...], preferred_element_type=F32).astype(BF16)
        push(g_send.at[j], g.at[x, g_rows(hour)], g_sem.at[0], g_sem.at[1], dev_x(j))

    def own_factor():
        g[x] = jnp.dot(p[quarter(x), :], onehot[...], preferred_element_type=F32).astype(BF16)
        locals_in[3].wait()
        locals_in[4].wait()

        def ramps(k, carry):
            index = lax.rem(hour * hours + k, 2 * hours)
            inner = (index != 0).astype(F32)
            row = 2.0 * ramp_weight[...] * (ramp[pl.ds(index, 1), :].astype(F32) * inner)
            rw[k] = jnp.broadcast_to(row, (SCEN, n_units))
            return carry

        lax.fori_loop(0, hours + 1, ramps, 0)
        halo().wait()

    def share_factors():
        take(g_send, g_sem.at[1])
        for j in range(3):
            part = g.at[at(x, j), g_rows(hour)]
            push(part, part, g_sem.at[2], g_sem.at[3], sibling)

    def halo():
        return pltpu.make_async_remote_copy(
            src_ref=gx.at[hours - (hours - 1) * hour], dst_ref=gx.at[(hours + 1) * hour],
            send_sem=halo_sem.at[0], recv_sem=halo_sem.at[1], device_id=sibling, device_id_type=MESH,
        )

    locals_in = [
        pltpu.make_async_copy(src, dst, in_sem.at[n])
        for n, (src, dst) in enumerate(
            [
                (commit_hbm, commit),
                (units_hbm, units),
                (load_hbm, load),
                (active_hbm, active.at[:, pl.ds(0, lines)]),
                (ramp_hbm, ramp),
                (limit_hbm, lim.at[0, pl.ds(0, lines)]),
                (weight_hbm, wgt.at[0, pl.ds(0, lines)]),
            ]
        )
    ]
    for dma in locals_in[:2]:
        dma.start()
    for k in range(4):
        fetch(lax.rem(x + (2, 1, 3, 0)[k], 4), lambda dma: dma.start())
        if k == 0:
            locals_in[2].start()
    for dma in locals_in[3:]:
        dma.start()
    barrier = pltpu.get_barrier_semaphore()
    for j in range(3):
        for dev in (dev_x(j), dev_y(j), dev_z(j)):
            pl.semaphore_signal(barrier, inc=1, device_id=dev, device_id_type=MESH)
    pl.semaphore_signal(barrier, inc=1, device_id=sibling, device_id_type=MESH)

    fill = 4 * QUARTER - lines
    p[lines:, :] = jnp.zeros((fill, nodes), BF16)
    active[:, lines:] = jnp.zeros((hours, fill), jnp.int32)
    lim[:, lines:] = jnp.zeros((1, fill), F32)
    wgt[:, lines:] = jnp.zeros((1, fill), F32)
    onehot[...] = (
        lax.broadcasted_iota(jnp.int32, onehot.shape, 0) == node[...] - bus * nodes
    ).astype(F32).astype(BF16)
    gx[(hours + 1) * hour] = jnp.zeros((SCEN, n_units), F32)
    locals_in[0].wait()
    locals_in[1].wait()

    def generate(k, carry):
        row = commit[pl.ds(k, 1), :]
        value = jnp.zeros((1, n_units), F32)
        for n in range(levels.shape[0]):
            value = value + jnp.where(row == n, levels[n], 0.0)
        value = jnp.broadcast_to(value, (SCEN, n_units))
        lev[k] = value
        gx[k + 1] = value * units[k]
        return carry

    lax.fori_loop(0, hours, generate, 0)
    locals_in[2].wait()

    steps = dict(zip("FR123456", (forward, relay, step1, step2, step3, step4, step5, step6)))

    def iteration(i, carry):
        for name, lag in ORDER:
            if name == "2":
                @pl.when(i == lag)
                def _():
                    locals_in[5].wait()
                    locals_in[6].wait()
            if name == "3":
                @pl.when(i == lag)
                def _():
                    share_factors()

            @pl.when((i >= lag) & (i < CHUNKS + lag))
            def _():
                steps[name](i - lag)

            if name == "F":
                @pl.when(i == 0)
                def _():
                    halo().start()
                    for j in (2, 0, 1):
                        send_factor(j)
                    own_factor()

        return carry

    lax.fori_loop(0, CHUNKS + max(lag for _, lag in ORDER), iteration, 0)
    take(part_a.at[pl.ds(0, 3)], ssem.at[OA])
    take(part_b.at[pl.ds(0, 3)], ssem.at[OB])
    take(land2_a, ssem.at[S2A])
    take(land2_b, ssem.at[S2B])
    take(fg.at[pl.ds(0, 3 * (columns // 4))], ssem.at[AGY])
    take(land_z, ssem.at[SUMZ])
    take(land_x, ssem.at[SUMX])
    take(land_x, ssem.at[AGZ])
    take(g_send, g_sem.at[0])
    take(g_send, g_sem.at[2])


def body(
    ptdf, units_out, load, unit_node, commit_index, relax_levels,
    line_active, line_limit, line_weight, ramp_active, ramp_limit, ramp_weight,
):
    hours, scen, units = units_out.shape
    lines, nodes = ptdf.shape
    columns = hours * scen
    vmem = pl.BlockSpec(memory_space=pltpu.VMEM)
    smem = pl.BlockSpec(memory_space=pltpu.SMEM)
    anywhere = pl.BlockSpec(memory_space=pl.ANY)
    dma = pltpu.SemaphoreType.DMA
    all_lines = 4 * QUARTER
    own = columns // 4
    grad = pl.pallas_call(
        kernel,
        out_shape=jax.ShapeDtypeStruct((columns, units), F32),
        in_specs=[smem] + [anywhere] * 8 + [vmem] * 3,
        out_specs=vmem,
        scratch_shapes=[
            pltpu.VMEM((all_lines, nodes), BF16),
            pltpu.VMEM((columns, nodes), F32),
            pltpu.VMEM((hours, scen, units), F32),
            pltpu.VMEM((hours, units), jnp.int32),
            pltpu.VMEM((hours, all_lines), jnp.int32),
            pltpu.VMEM((2 * hours, units), jnp.int32),
            pltpu.VMEM((hours, scen, units), F32),
            pltpu.VMEM((hours + 2, scen, units), F32),
            pltpu.VMEM((hours + 1, scen, units), F32),
            pltpu.VMEM((1, all_lines), F32),
            pltpu.VMEM((1, all_lines), F32),
            pltpu.VMEM((columns // CHUNKS, nodes), BF16),
            pltpu.VMEM((4, columns, HALF), BF16),
            pltpu.VMEM((4, columns, HALF), BF16),
            pltpu.VMEM((columns, HALF), F32),
            pltpu.VMEM((columns, HALF), BF16),
            pltpu.VMEM((4, own, HALF), BF16),
            pltpu.VMEM((2, columns, HALF), BF16),
            pltpu.VMEM((2, 4, own, HALF), BF16),
            pltpu.VMEM((columns, HALF), BF16),
            pltpu.VMEM((4, own, HALF), BF16),
            pltpu.VMEM((3, own, HALF), BF16),
            pltpu.VMEM((3, own, HALF), BF16),
            pltpu.VMEM((columns, QUARTER), BF16),
            pltpu.VMEM((columns, 4 * units), F32),
            pltpu.VMEM((columns, 4 * units), BF16),
            pltpu.VMEM((3, own, 4 * units), BF16),
            pltpu.VMEM((own, 4 * units), F32),
            pltpu.VMEM((3, own, units), F32),
            pltpu.VMEM((columns, units), F32),
            pltpu.VMEM((nodes, units), BF16),
            pltpu.VMEM((3, HALF, units), BF16),
            pltpu.VMEM((4, QUARTER, units), BF16),
            dma((4,)),
            dma((7,)),
            dma((KINDS,)),
            dma((KINDS, CHUNKS)),
            dma((4,)),
            dma((2,)),
        ],
        compiler_params=pltpu.CompilerParams(
            collective_id=0, has_side_effects=True, vmem_limit_bytes=62 << 20
        ),
    )(
        relax_levels, ptdf, load.reshape(columns, nodes), units_out, commit_index, line_active,
        ramp_active, line_limit, line_weight, unit_node[None, :], ramp_limit[None, :],
        ramp_weight[None, :],
    )
    return grad.reshape(hours, scen, units)


def solution(mesh):
    return jax.shard_map(
        body,
        mesh=mesh,
        in_specs=(
            P("line", "bus"),
            P("hour", None, "bus"),
            P("hour", None, "bus"),
            P("bus"),
            P("hour", "bus"),
            P(),
            P("hour", "line"),
            P("line"),
            P("line"),
            P(None, "bus"),
            P("bus"),
            P("bus"),
        ),
        out_specs=P("hour", None, "bus"),
        check_vma=False,
    )
```

```python
import jax
import jax.numpy as jnp
from jax import lax
from jax.experimental import pallas as pl
from jax.experimental.pallas import tpu as pltpu
from jax.sharding import PartitionSpec as P

MESH = pl.DeviceIdType.MESH
F32 = jnp.float32
BF16 = jnp.bfloat16

CHUNKS = 6
TOGETHER = 2
QUARTER = 1280
SIDE_A = 512
SIDE_B = QUARTER - SIDE_A
HALF = QUARTER // 2
SCEN = 8
OA, OB, TA, TB, S2A, S2B, AGY, AGR, SUMZ, SUMX, AGZ = range(11)
KINDS = 11
ORDER = (("F", 0), ("Y", 6), ("2", 5), ("5", 10), ("4", 8), ("1", 3), ("3", 6), ("R", 1), ("6", 11))
FACTORS = (1, 3, 2, 5)


def hinge_grad(values, limits):
    return jnp.maximum(values - limits, 0.0) - jnp.maximum(-values - limits, 0.0)


def kernel(
    levels, ptdf_hbm, load_hbm, units_hbm, commit_hbm, active_hbm, ramp_hbm, limit_hbm, weight_hbm,
    node, ramp_limit, ramp_weight, out,
    p, load, units, commit, active, ramp, lev, gx, rw, lim, wgt, inj,
    part_a, part_b, own_a, relay_a, relay_b, land_a, land_b, sum_a, sum_b, land2_a, land2_b,
    fg, u, u_send, land_z, sum_z, land_x, ob, onehot, g_send, g,
    p_sem, in_sem, ssem, rsem, g_sem, halo_sem,
):
    columns, nodes = load.shape
    hours = columns // SCEN
    lines = ptdf_hbm.shape[0]
    n_units = node.shape[1]
    chunk = columns // CHUNKS
    sub = chunk // 4
    block = chunk * TOGETHER
    hour = lax.axis_index("hour")
    bus = lax.axis_index("bus")
    z = lax.axis_index("line")
    x = bus // 4
    y = bus % 4
    sibling = (1 - hour, bus, z)

    def at(pos, j):
        return lax.rem(pos + (1, 3, 2)[j], 4)

    def dev_x(j):
        return (hour, at(x, j) * 4 + y, z)

    def dev_y(j):
        return (hour, x * 4 + at(y, j), z)

    def dev_z(j):
        return (hour, bus, at(z, j))

    def span(start, size):
        return pl.ds(pl.multiple_of(start, size), size)

    def rows(c):
        return span(c * chunk, chunk)

    def own(c):
        return span(c * sub, sub)

    def rows_of(c, pos):
        return span(c * chunk + pos * sub, sub)

    def half_rows(c, h):
        return span(c * chunk + h * (chunk // 2), chunk // 2)

    def own_rows(c, times):
        return pl.ds(pl.multiple_of(c * chunk, chunk), times * sub)

    def over_rows(start, size, step, work):
        @pl.loop(0, size // step)
        def _(k):
            work(span(start + k * step, step))

    def quarter(q):
        return pl.ds(pl.multiple_of(q * QUARTER, QUARTER), QUARTER)

    def unit_lanes(pos):
        return pl.ds(pl.multiple_of(pos * n_units, n_units), n_units)

    def push(src, dst, send_sem, recv_sem, dev):
        pltpu.make_async_remote_copy(
            src_ref=src, dst_ref=dst, send_sem=send_sem, recv_sem=recv_sem,
            device_id=dev, device_id_type=MESH,
        ).start()

    def take(ref, sem):
        pltpu.make_async_copy(ref, ref, sem).wait()

    def receive(kind, c, ref):
        take(ref, rsem.at[kind, c])

    def fetch(q, do):
        last = lines - 3 * QUARTER

        @pl.when(q < 3)
        def _():
            do(pltpu.make_async_copy(ptdf_hbm.at[quarter(q)], p.at[quarter(q)], p_sem.at[q]))

        @pl.when(q == 3)
        def _():
            part = pl.ds(3 * QUARTER, last)
            do(pltpu.make_async_copy(ptdf_hbm.at[part], p.at[part], p_sem.at[3]))

    def injection(c):
        per = block // SCEN
        rest = gx[pl.ds(1 + c * (chunk // SCEN), per)].reshape(block, n_units)
        placed = None
        for _ in range(3):
            head = rest.astype(BF16)
            rest = rest - head.astype(F32)
            term = lax.dot_general(
                head, onehot[...], (((1,), (1,)), ((), ())), preferred_element_type=F32
            )
            placed = term if placed is None else placed + term
        where = pl.ds(pl.multiple_of(c * chunk, chunk), block)
        inj[...] = (placed - load[where, :]).astype(BF16)

    def product(start, size):
        where = pl.ds(pl.multiple_of(start, 128), size)
        return lax.dot_general(
            inj[...], p[where, :], (((1,), (1,)), ((), ())), preferred_element_type=F32
        )

    def send_far_a(c):
        for j in range(2):
            push(part_a.at[at(x, 2), half_rows(c, j)], relay_a.at[half_rows(c, j)],
                 ssem.at[OA], rsem.at[OA, c], dev_x(j))

    def send_near_a(c, j):
        half = half_rows(c, 1 - j)
        push(part_a.at[at(x, j), half], land_a.at[j, half], ssem.at[OA], rsem.at[TA, c], dev_x(j))

    def send_b(c, q):
        side = q // 2
        far = lax.rem(y + 1 + 2 * side, 4)
        push(part_b.at[q, rows_of(c, at(y, 2))], relay_b.at[q, own(c)],
             ssem.at[OB], rsem.at[OB, c], (hour, x * 4 + far, z))
        near = lax.rem(y + 3 - 2 * side, 4)
        push(part_b.at[q, rows_of(c, near)], land_b.at[1 - side, q, own(c)],
             ssem.at[OB], rsem.at[TB, c], (hour, x * 4 + near, z))

    def multiply(c):
        injection(c)
        where = pl.ds(pl.multiple_of(c * chunk, chunk), block)

        @pl.loop(0, 4)
        def _(k):
            q = lax.rem(x + 2 + k, 4)

            @pl.when(c == 0)
            def _():
                fetch(q, lambda dma: dma.wait())

            flow = product(q * QUARTER, SIDE_A)
            part_a[q, where] = flow.astype(BF16)

            @pl.when((c == 0) & (k == 0))
            def _():
                pl.semaphore_wait(pltpu.get_barrier_semaphore(), 10)

            @pl.when(k == 0)
            def _():
                send_far_a(c)

            @pl.when(k == 1)
            def _():
                send_near_a(c, 1)

            @pl.when(k == 2)
            def _():
                own_a[where] = flow

            @pl.when(k == 3)
            def _():
                send_near_a(c, 0)

            part_b[q, where] = product(q * QUARTER + SIDE_A, SIDE_B).astype(BF16)
            send_b(c, q)

    def forward(c):
        if TOGETHER == 1:
            multiply(c)
            return

        @pl.when(lax.rem(c, TOGETHER) == 0)
        def _():
            multiply(c)

        @pl.when(lax.rem(c, TOGETHER) != 0)
        def _():
            send_far_a(c)

            @pl.loop(0, 4)
            def _(q):
                send_b(c, q)

            for j in range(2):
                send_near_a(c, j)

    def relay(c):
        receive(OA, c, relay_a.at[rows(c)])
        for j in range(2):
            q = at(x, j)

            def add_a(where):
                part_a[q, where, :] = (
                    part_a[q, where, :].astype(F32) + relay_a[where, :].astype(F32)
                ).astype(BF16)

            over_rows(c * chunk + j * (chunk // 2), chunk // 2, 16, add_a)
            half = half_rows(c, j)
            push(part_a.at[q, half], land_a.at[j, half], ssem.at[OA], rsem.at[TA, c], dev_x(j))
        receive(OB, c, relay_b.at[:, own(c)])
        for j in range(2):
            where = rows_of(c, at(y, j))

            @pl.loop(2 * j, 2 * j + 2)
            def _(q):
                part_b[q, where, :] = (
                    part_b[q, where, :].astype(F32) + relay_b[q, own(c), :].astype(F32)
                ).astype(BF16)

            pair = pl.ds(2 * j, 2)
            push(part_b.at[pair, where], land_b.at[j, pair, own(c)],
                 ssem.at[OB], rsem.at[TB, c], dev_y(j))

    def total_a(where):
        return own_a[where, :] + land_a[0, where, :].astype(F32) + land_a[1, where, :].astype(F32)

    def total_b(c, q):
        total = part_b[q, rows_of(c, y), :].astype(F32)
        for j in range(2):
            total = total + land_b[j, q, own(c), :].astype(F32)
        return total

    def step1(c):
        receive(TA, c, land_a.at[:, rows(c)])

        def add_a(where):
            sum_a[where, :] = total_a(where).astype(BF16)

        over_rows(c * chunk, chunk, 16, add_a)
        for j in (2, 0, 1):
            push(sum_a.at[rows_of(c, at(y, j))], land2_a.at[j, own(c)],
                 ssem.at[S2A], rsem.at[S2A, c], dev_y(j))
        receive(TB, c, land_b.at[:, :, own(c)])

        @pl.loop(0, 4)
        def _(q):
            sum_b[q, own(c), :] = total_b(c, q).astype(BF16)

        for j in (2, 0, 1):
            push(sum_b.at[at(x, j), own(c)], land2_b.at[j, own(c)],
                 ssem.at[S2B], rsem.at[S2B, c], dev_x(j))

    def step2(c):
        per = sub // SCEN
        line = quarter(x)
        mask = jnp.concatenate(
            [
                jnp.broadcast_to(
                    active[pl.ds((c * 4 + y) * per + k, 1), line].astype(F32), (SCEN, QUARTER)
                )
                for k in range(per)
            ],
            axis=0,
        )
        scale = 2.0 * wgt[:, line] * mask
        bound = lim[:, line]
        where = rows_of(c, y)
        receive(S2A, c, land2_a.at[:, own(c)])
        total = total_a(where)
        for j in range(3):
            total = total + land2_a[j, own(c), :].astype(F32)
        fg[where, 0:SIDE_A] = (
            scale[:, 0:SIDE_A] * hinge_grad(total, bound[:, 0:SIDE_A])
        ).astype(BF16)
        receive(S2B, c, land2_b.at[:, own(c)])
        total = total_b(c, x)
        for j in range(3):
            total = total + land2_b[j, own(c), :].astype(F32)
        fg[where, SIDE_A:QUARTER] = (
            scale[:, SIDE_A:QUARTER] * hinge_grad(total, bound[:, SIDE_A:QUARTER])
        ).astype(BF16)
        for j in range(2):
            push(fg.at[where], fg.at[where], ssem.at[AGY], rsem.at[AGY, c], dev_y(j))

    def gather_relay(c):
        receive(AGY, c, fg.at[own_rows(c, 2)])
        for j in range(2):
            part = fg.at[rows_of(c, at(y, 1 - j)), pl.ds(j * HALF, HALF)]
            push(part, part, ssem.at[AGY], rsem.at[AGR, c], dev_y(j))

    def step3(c):
        @pl.when(c == 0)
        def _():
            take(g_send, g_sem.at[3])

        receive(AGR, c, fg.at[own_rows(c, 1)])

        @pl.loop(0, 4)
        def _(k):
            grad = jnp.dot(fg[rows(c), :], g[k], preferred_element_type=F32)
            u[rows(c), unit_lanes(k)] = grad
            u_send[rows(c), unit_lanes(k)] = grad.astype(BF16)

        for j in (2, 0, 1):
            push(u_send.at[rows_of(c, at(z, j))], land_z.at[j, own(c)],
                 ssem.at[SUMZ], rsem.at[SUMZ, c], dev_z(j))

    def step4(c):
        receive(SUMZ, c, land_z.at[:, own(c)])

        @pl.loop(0, 4)
        def _(k):
            total = u[rows_of(c, z), unit_lanes(k)]
            for j in range(3):
                total = total + land_z[j, own(c), unit_lanes(k)].astype(F32)
            sum_z[own(c), unit_lanes(k)] = total

        for j in (2, 0, 1):
            push(sum_z.at[own(c), unit_lanes(at(x, j))], land_x.at[j, own(c)],
                 ssem.at[SUMX], rsem.at[SUMX, c], dev_x(j))

    def step5(c):
        receive(SUMX, c, land_x.at[:, own(c)])
        total = sum_z[own(c), unit_lanes(x)]
        for j in range(3):
            total = total + land_x[j, own(c), :]
        where = rows_of(c, z)
        ob[where, :] = total
        for j in (2, 0, 1):
            push(ob.at[where], ob.at[where], ssem.at[AGZ], rsem.at[AGZ, c], dev_z(j))

    def step6(c):
        receive(AGZ, c, ob.at[own_rows(c, 3)])
        per = chunk // SCEN
        bound = ramp_limit[...][None]

        @pl.loop(0, per // 4)
        def _(k):
            h = c * per + k * 4
            step = gx[pl.ds(h + 1, 5)] - gx[pl.ds(h, 5)]
            dual = rw[pl.ds(h, 5)] * hinge_grad(step, bound)
            where = span(h * SCEN, 4 * SCEN)
            grad = ob[where, :].reshape(4, SCEN, n_units) + dual[:-1] - dual[1:]
            out[where, :] = (lev[pl.ds(h, 4)] * grad).reshape(4 * SCEN, n_units)

    def g_rows(h):
        return pl.ds(pl.multiple_of(h * HALF, HALF), HALF)

    def send_factor(j):
        where = pl.ds(pl.multiple_of(at(x, j) * QUARTER + hour * HALF, HALF), HALF)
        g_send[j] = jnp.dot(p[where, :], onehot[...], preferred_element_type=F32).astype(BF16)
        push(g_send.at[j], g.at[x, g_rows(hour)], g_sem.at[0], g_sem.at[1], dev_x(j))

    def own_factor():
        g[x] = jnp.dot(p[quarter(x), :], onehot[...], preferred_element_type=F32).astype(BF16)
        locals_in[3].wait()
        locals_in[4].wait()

        def ramps(k, carry):
            index = lax.rem(hour * hours + k, 2 * hours)
            inner = (index != 0).astype(F32)
            row = 2.0 * ramp_weight[...] * (ramp[pl.ds(index, 1), :].astype(F32) * inner)
            rw[k] = jnp.broadcast_to(row, (SCEN, n_units))
            return carry

        lax.fori_loop(0, hours + 1, ramps, 0)
        halo().wait()

    def share_factors():
        take(g_send, g_sem.at[1])
        for j in range(3):
            part = g.at[at(x, j), g_rows(hour)]
            push(part, part, g_sem.at[2], g_sem.at[3], sibling)

    def halo():
        return pltpu.make_async_remote_copy(
            src_ref=gx.at[hours - (hours - 1) * hour], dst_ref=gx.at[(hours + 1) * hour],
            send_sem=halo_sem.at[0], recv_sem=halo_sem.at[1], device_id=sibling, device_id_type=MESH,
        )

    locals_in = [
        pltpu.make_async_copy(src, dst, in_sem.at[n])
        for n, (src, dst) in enumerate(
            [
                (commit_hbm, commit),
                (units_hbm, units),
                (load_hbm, load),
                (active_hbm, active.at[:, pl.ds(0, lines)]),
                (ramp_hbm, ramp),
                (limit_hbm, lim.at[0, pl.ds(0, lines)]),
                (weight_hbm, wgt.at[0, pl.ds(0, lines)]),
            ]
        )
    ]
    for dma in locals_in[:2]:
        dma.start()
    for k in range(4):
        fetch(lax.rem(x + (2, 1, 3, 0)[k], 4), lambda dma: dma.start())
        if k == 0:
            locals_in[2].start()
    for dma in locals_in[3:]:
        dma.start()
    barrier = pltpu.get_barrier_semaphore()
    for j in range(3):
        for dev in (dev_x(j), dev_y(j), dev_z(j)):
            pl.semaphore_signal(barrier, inc=1, device_id=dev, device_id_type=MESH)
    pl.semaphore_signal(barrier, inc=1, device_id=sibling, device_id_type=MESH)

    fill = 4 * QUARTER - lines
    p[lines:, :] = jnp.zeros((fill, nodes), BF16)
    active[:, lines:] = jnp.zeros((hours, fill), jnp.int32)
    lim[:, lines:] = jnp.zeros((1, fill), F32)
    wgt[:, lines:] = jnp.zeros((1, fill), F32)
    onehot[...] = (
        lax.broadcasted_iota(jnp.int32, onehot.shape, 0) == node[...] - bus * nodes
    ).astype(F32).astype(BF16)
    gx[(hours + 1) * hour] = jnp.zeros((SCEN, n_units), F32)
    locals_in[0].wait()
    locals_in[1].wait()

    def generate(k, carry):
        row = commit[pl.ds(k, 1), :]
        value = jnp.zeros((1, n_units), F32)
        for n in range(levels.shape[0]):
            value = value + jnp.where(row == n, levels[n], 0.0)
        value = jnp.broadcast_to(value, (SCEN, n_units))
        lev[k] = value
        gx[k + 1] = value * units[k]
        return carry

    lax.fori_loop(0, hours, generate, 0)
    locals_in[2].wait()

    steps = dict(
        F=forward, R=relay, Y=gather_relay,
        **dict(zip("123456", (step1, step2, step3, step4, step5, step6))),
    )

    def iteration(i, carry):
        for name, lag in ORDER:
            if name == "2":
                @pl.when(i == lag)
                def _():
                    locals_in[5].wait()
                    locals_in[6].wait()
            @pl.when((i >= lag) & (i < CHUNKS + lag))
            def _():
                steps[name](i - lag)

            if name == "F":
                @pl.when(i == 0)
                def _():
                    halo().start()
                    own_factor()

        for j in (2, 0, 1):
            @pl.when(i == FACTORS[j])
            def _():
                send_factor(j)

        @pl.when(i == FACTORS[3])
        def _():
            share_factors()

        return carry

    lax.fori_loop(0, CHUNKS + max(lag for _, lag in ORDER), iteration, 0)
    take(part_a.at[pl.ds(0, 3)], ssem.at[OA])
    take(part_b.at[pl.ds(0, 3)], ssem.at[OB])
    take(land2_a, ssem.at[S2A])
    take(land2_b, ssem.at[S2B])
    take(fg.at[pl.ds(0, 3 * (columns // 4))], ssem.at[AGY])
    take(land_z, ssem.at[SUMZ])
    take(land_x, ssem.at[SUMX])
    take(land_x, ssem.at[AGZ])
    take(g_send, g_sem.at[0])
    take(g_send, g_sem.at[2])


def body(
    ptdf, units_out, load, unit_node, commit_index, relax_levels,
    line_active, line_limit, line_weight, ramp_active, ramp_limit, ramp_weight,
):
    hours, scen, units = units_out.shape
    lines, nodes = ptdf.shape
    columns = hours * scen
    vmem = pl.BlockSpec(memory_space=pltpu.VMEM)
    smem = pl.BlockSpec(memory_space=pltpu.SMEM)
    anywhere = pl.BlockSpec(memory_space=pl.ANY)
    dma = pltpu.SemaphoreType.DMA
    all_lines = 4 * QUARTER
    own = columns // 4
    grad = pl.pallas_call(
        kernel,
        out_shape=jax.ShapeDtypeStruct((columns, units), F32),
        in_specs=[smem] + [anywhere] * 8 + [vmem] * 3,
        out_specs=vmem,
        scratch_shapes=[
            pltpu.VMEM((all_lines, nodes), BF16),
            pltpu.VMEM((columns, nodes), F32),
            pltpu.VMEM((hours, scen, units), F32),
            pltpu.VMEM((hours, units), jnp.int32),
            pltpu.VMEM((hours, all_lines), jnp.int32),
            pltpu.VMEM((2 * hours, units), jnp.int32),
            pltpu.VMEM((hours, scen, units), F32),
            pltpu.VMEM((hours + 2, scen, units), F32),
            pltpu.VMEM((hours + 1, scen, units), F32),
            pltpu.VMEM((1, all_lines), F32),
            pltpu.VMEM((1, all_lines), F32),
            pltpu.VMEM((columns // CHUNKS * TOGETHER, nodes), BF16),
            pltpu.VMEM((4, columns, SIDE_A), BF16),
            pltpu.VMEM((4, columns, SIDE_B), BF16),
            pltpu.VMEM((columns, SIDE_A), F32),
            pltpu.VMEM((columns, SIDE_A), BF16),
            pltpu.VMEM((4, own, SIDE_B), BF16),
            pltpu.VMEM((2, columns, SIDE_A), BF16),
            pltpu.VMEM((2, 4, own, SIDE_B), BF16),
            pltpu.VMEM((columns, SIDE_A), BF16),
            pltpu.VMEM((4, own, SIDE_B), BF16),
            pltpu.VMEM((3, own, SIDE_A), BF16),
            pltpu.VMEM((3, own, SIDE_B), BF16),
            pltpu.VMEM((columns, QUARTER), BF16),
            pltpu.VMEM((columns, 4 * units), F32),
            pltpu.VMEM((columns, 4 * units), BF16),
            pltpu.VMEM((3, own, 4 * units), BF16),
            pltpu.VMEM((own, 4 * units), F32),
            pltpu.VMEM((3, own, units), F32),
            pltpu.VMEM((columns, units), F32),
            pltpu.VMEM((nodes, units), BF16),
            pltpu.VMEM((3, HALF, units), BF16),
            pltpu.VMEM((4, QUARTER, units), BF16),
            dma((4,)),
            dma((7,)),
            dma((KINDS,)),
            dma((KINDS, CHUNKS)),
            dma((4,)),
            dma((2,)),
        ],
        compiler_params=pltpu.CompilerParams(
            collective_id=0, has_side_effects=True, vmem_limit_bytes=62 << 20
        ),
    )(
        relax_levels, ptdf, load.reshape(columns, nodes), units_out, commit_index, line_active,
        ramp_active, line_limit, line_weight, unit_node[None, :], ramp_limit[None, :],
        ramp_weight[None, :],
    )
    return grad.reshape(hours, scen, units)


def solution(mesh):
    return jax.shard_map(
        body,
        mesh=mesh,
        in_specs=(
            P("line", "bus"),
            P("hour", None, "bus"),
            P("hour", None, "bus"),
            P("bus"),
            P("hour", "bus"),
            P(),
            P("hour", "line"),
            P("line"),
            P("line"),
            P(None, "bus"),
            P("bus"),
            P("bus"),
        ),
        out_specs=P("hour", None, "bus"),
        check_vma=False,
    )
```

```python
import jax
import jax.numpy as jnp
from jax import lax
from jax.experimental import pallas as pl
from jax.experimental.pallas import tpu as pltpu
from jax.sharding import PartitionSpec as P

MESH = pl.DeviceIdType.MESH
F32 = jnp.float32
BF16 = jnp.bfloat16

CHUNKS = 6
TOGETHER = 2
QUARTER = 1280
SIDE_A = 640
SIDE_B = QUARTER - SIDE_A
HALF = QUARTER // 2
SCEN = 8
OA, OB, TA, TB, S2A, S2B, AGY, AGR, SUMZ, SUMX, AGZ, SCALE = range(12)
KINDS = 15
ORDER = (("F", 0), ("2", 5), ("5", 9), ("1", 3), ("R", 1), ("3", 6), ("6", 12), ("Y", 5), ("4", 7))
FACTORS = (2, 3, 5)


def hinge_grad(values, limits):
    return jnp.maximum(values - limits, 0.0) - jnp.maximum(-values - limits, 0.0)


def kernel(
    levels, ptdf_hbm, load_hbm, units_hbm, commit_hbm, active_hbm, ramp_hbm, limit_hbm, weight_hbm,
    node, ramp_limit, ramp_weight, out,
    p, load, units, commit, active, ramp, lev, gx, rw, lim, wgt, inj,
    part_a, part_b, own_a, near_a, prod_b, own_b, near_b, relay_a, relay_b, land_a, land_b, sum_a, sum_b, code_a, code_b, land2_a, land2_b,
    scale, land_scale, fg, u, code_u, land_z, sum_z, land_x, ob, onehot, g_send, g,
    p_sem, in_sem, ssem, rsem, g_sem, halo_sem,
):
    columns, nodes = load.shape
    hours = columns // SCEN
    lines = ptdf_hbm.shape[0]
    n_units = node.shape[1]
    chunk = columns // CHUNKS
    sub = chunk // 4
    block = chunk * TOGETHER
    hour = lax.axis_index("hour")
    bus = lax.axis_index("bus")
    z = lax.axis_index("line")
    x = bus // 4
    y = bus % 4
    sibling = (1 - hour, bus, z)

    def at(pos, j):
        return lax.rem(pos + (1, 3, 2)[j], 4)

    def dev_x(j):
        return (hour, at(x, j) * 4 + y, z)

    def dev_y(j):
        return (hour, x * 4 + at(y, j), z)

    def dev_z(j):
        return (hour, bus, at(z, j))

    def span(start, size):
        return pl.ds(pl.multiple_of(start, size), size)

    def rows(c):
        return span(c * chunk, chunk)

    def own(c):
        return span(c * sub, sub)

    def rows_of(c, pos):
        return span(c * chunk + pos * sub, sub)

    def half_rows(c, h):
        return span(c * chunk + h * (chunk // 2), chunk // 2)

    def own_rows(c, times):
        return pl.ds(pl.multiple_of(c * chunk, chunk), times * sub)

    def over_rows(start, size, step, work):
        @pl.loop(0, size // step)
        def _(k):
            work(span(start + k * step, step))

    def quarter(q):
        return pl.ds(pl.multiple_of(q * QUARTER, QUARTER), QUARTER)

    def unit_lanes(pos):
        return pl.ds(pl.multiple_of(pos * n_units, n_units), n_units)

    def push(src, dst, send_sem, recv_sem, dev):
        pltpu.make_async_remote_copy(
            src_ref=src, dst_ref=dst, send_sem=send_sem, recv_sem=recv_sem,
            device_id=dev, device_id_type=MESH,
        ).start()

    def take(ref, sem):
        pltpu.make_async_copy(ref, ref, sem).wait()

    def receive(kind, c, ref):
        take(ref, rsem.at[kind, c])

    def fetch(q, do):
        last = lines - 3 * QUARTER

        @pl.when(q < 3)
        def _():
            do(pltpu.make_async_copy(ptdf_hbm.at[quarter(q)], p.at[quarter(q)], p_sem.at[q]))

        @pl.when(q == 3)
        def _():
            part = pl.ds(3 * QUARTER, last)
            do(pltpu.make_async_copy(ptdf_hbm.at[part], p.at[part], p_sem.at[3]))

    def injection(c):
        per = block // SCEN
        rest = gx[pl.ds(1 + c * (chunk // SCEN), per)].reshape(block, n_units)
        placed = None
        for _ in range(3):
            head = rest.astype(BF16)
            rest = rest - head.astype(F32)
            term = lax.dot_general(
                head, onehot[...], (((1,), (1,)), ((), ())), preferred_element_type=F32
            )
            placed = term if placed is None else placed + term
        where = pl.ds(pl.multiple_of(c * chunk, chunk), block)
        inj[...] = (placed - load[where, :]).astype(BF16)

    def product(start, size):
        where = pl.ds(pl.multiple_of(start, 128), size)
        return lax.dot_general(
            inj[...], p[where, :], (((1,), (1,)), ((), ())), preferred_element_type=F32
        )

    def send_far_a(c):
        for j in range(2):
            push(part_a.at[at(x, 2), half_rows(c, j)], relay_a.at[half_rows(c, j)],
                 ssem.at[OA], rsem.at[OA, c], dev_x(j))

    def send_near_a(c, j):
        half = half_rows(c, 1 - j)
        push(part_a.at[at(x, j), half], land_a.at[j, half], ssem.at[OA], rsem.at[TA, c], dev_x(j))

    def send_b(c, q):
        side = q // 2
        far = lax.rem(y + 1 + 2 * side, 4)
        push(part_b.at[q, rows_of(c, at(y, 2))], relay_b.at[q, own(c)],
             ssem.at[OB], rsem.at[OB, c], (hour, x * 4 + far, z))
        near = lax.rem(y + 3 - 2 * side, 4)
        push(part_b.at[q, rows_of(c, near)], land_b.at[1 - side, q, own(c)],
             ssem.at[OB], rsem.at[TB, c], (hour, x * 4 + near, z))

    def multiply(c):
        injection(c)
        where = pl.ds(pl.multiple_of(c * chunk, chunk), block)

        @pl.loop(0, 4)
        def _(k):
            q = lax.rem(x + 2 + k, 4)

            @pl.when((c == 0) & (k > 0))
            def _():
                fetch(q, lambda dma: dma.wait())

            flow = product(q * QUARTER, SIDE_A)
            part_a[q, where] = flow.astype(BF16)

            @pl.when(k == 0)
            def _():
                send_far_a(c)

            def keep(j):
                for n in range(TOGETHER):
                    low = n * chunk + j * (chunk // 2)
                    near_a[half_rows(c + n, j), :] = flow[low : low + chunk // 2, :]

            @pl.when(k == 1)
            def _():
                keep(1)
                send_near_a(c, 1)

            @pl.when(k == 2)
            def _():
                own_a[where] = flow

            @pl.when(k == 3)
            def _():
                keep(0)
                send_near_a(c, 0)

            flow_b = product(q * QUARTER + SIDE_A, SIDE_B)
            part_b[q, where] = flow_b.astype(BF16)
            send_b(c, q)
            prod_b[...] = flow_b
            beside = lax.rem(y + 1 + 2 * (q // 2), 4)
            for n in range(TOGETHER):
                own_b[q, own(c + n), :] = prod_b[span(n * chunk + y * sub, sub), :]
                near_b[q, own(c + n), :] = prod_b[span(n * chunk + beside * sub, sub), :]

    def forward(c):
        if TOGETHER == 1:
            multiply(c)
            return

        @pl.when(lax.rem(c, TOGETHER) == 0)
        def _():
            multiply(c)

        @pl.when(lax.rem(c, TOGETHER) != 0)
        def _():
            send_far_a(c)

            @pl.loop(0, 4)
            def _(q):
                send_b(c, q)

            for j in range(2):
                send_near_a(c, j)

    def encode(n, c, values):
        most = jnp.maximum(jnp.max(jnp.abs(values), keepdims=True).reshape(1, 1), 1e-30)
        scale[n, c] = jnp.broadcast_to(most / 32000.0, (8, 128))
        return 32000.0 / most

    def coded(values, factor):
        return jnp.round(values * factor).astype(jnp.int32).astype(jnp.int16)

    def decode(n, j, c, codes):
        return codes.astype(jnp.int32).astype(F32) * land_scale[n, j, c, 0:1, 0:1]

    def send_scale(n, c, j, dev):
        push(scale.at[n, c], land_scale.at[n, j, c], ssem.at[SCALE + n], rsem.at[SCALE + n, c], dev)

    def receive_scale(n, c):
        receive(SCALE + n, c, land_scale.at[n, :, c])

    def relay(c):
        receive(OA, c, relay_a.at[rows(c)])
        for j in range(2):
            q = at(x, j)

            def add_a(where):
                part_a[q, where, :] = (
                    near_a[where, :] + relay_a[where, :].astype(F32)
                ).astype(BF16)

            over_rows(c * chunk + j * (chunk // 2), chunk // 2, 16, add_a)
            half = half_rows(c, j)
            push(part_a.at[q, half], land_a.at[j, half], ssem.at[OA], rsem.at[TA, c], dev_x(j))
        receive(OB, c, relay_b.at[:, own(c)])
        for j in range(2):
            where = rows_of(c, at(y, j))

            @pl.loop(2 * j, 2 * j + 2)
            def _(q):
                part_b[q, where, :] = (
                    near_b[q, own(c), :] + relay_b[q, own(c), :].astype(F32)
                ).astype(BF16)

            pair = pl.ds(2 * j, 2)
            push(part_b.at[pair, where], land_b.at[j, pair, own(c)],
                 ssem.at[OB], rsem.at[TB, c], dev_y(j))

    def total_a(where):
        return own_a[where, :] + land_a[0, where, :].astype(F32) + land_a[1, where, :].astype(F32)

    def total_b(c, q):
        total = own_b[q, own(c), :]
        for j in range(2):
            total = total + land_b[j, q, own(c), :].astype(F32)
        return total

    def step1(c):
        receive(TA, c, land_a.at[:, rows(c)])
        sum_a[...] = total_a(rows(c))
        factor = encode(0, c, sum_a[...])
        code_a[rows(c), :] = coded(sum_a[...], factor)
        for j in (2, 0, 1):
            send_scale(0, c, j, dev_y(j))
            push(code_a.at[rows_of(c, at(y, j))], land2_a.at[j, own(c)],
                 ssem.at[S2A], rsem.at[S2A, c], dev_y(j))
        receive(TB, c, land_b.at[:, :, own(c)])

        @pl.loop(0, 4)
        def _(q):
            sum_b[span(q * sub, sub), :] = total_b(c, q)

        factor_b = encode(1, c, sum_b[...])

        @pl.loop(0, 4)
        def _(q):
            code_b[q, own(c), :] = coded(sum_b[span(q * sub, sub), :], factor_b)

        for j in (2, 0, 1):
            send_scale(1, c, j, dev_x(j))
            push(code_b.at[at(x, j), own(c)], land2_b.at[j, own(c)],
                 ssem.at[S2B], rsem.at[S2B, c], dev_x(j))

    def step2(c):
        per = sub // SCEN
        line = quarter(x)
        mask = jnp.concatenate(
            [
                jnp.broadcast_to(
                    active[pl.ds((c * 4 + y) * per + k, 1), line].astype(F32), (SCEN, QUARTER)
                )
                for k in range(per)
            ],
            axis=0,
        )
        scale = 2.0 * wgt[:, line] * mask
        bound = lim[:, line]
        where = rows_of(c, y)
        receive_scale(0, c)
        receive(S2A, c, land2_a.at[:, own(c)])
        total = total_a(where)
        for j in range(3):
            total = total + decode(0, j, c, land2_a[j, own(c), :])
        fg[where, 0:SIDE_A] = (
            scale[:, 0:SIDE_A] * hinge_grad(total, bound[:, 0:SIDE_A])
        ).astype(BF16)
        receive_scale(1, c)
        receive(S2B, c, land2_b.at[:, own(c)])
        total = total_b(c, x)
        for j in range(3):
            total = total + decode(1, j, c, land2_b[j, own(c), :])
        fg[where, SIDE_A:QUARTER] = (
            scale[:, SIDE_A:QUARTER] * hinge_grad(total, bound[:, SIDE_A:QUARTER])
        ).astype(BF16)
        for j in range(2):
            push(fg.at[where], fg.at[where], ssem.at[AGY], rsem.at[AGY, c], dev_y(j))

    def gather_relay(c):
        receive(AGY, c, fg.at[own_rows(c, 2)])
        for j in range(2):
            part = fg.at[rows_of(c, at(y, 1 - j)), pl.ds(j * HALF, HALF)]
            push(part, part, ssem.at[AGY], rsem.at[AGR, c], dev_y(j))

    def step3(c):
        @pl.when(c == 0)
        def _():
            take(g_send, g_sem.at[3])

        receive(AGR, c, fg.at[own_rows(c, 1)])

        @pl.loop(0, 4)
        def _(k):
            u[rows(c), unit_lanes(k)] = jnp.dot(fg[rows(c), :], g[k], preferred_element_type=F32)

        factor = encode(2, c, u[rows(c), :])

        @pl.loop(0, 4)
        def _(k):
            code_u[rows(c), unit_lanes(k)] = coded(u[rows(c), unit_lanes(k)], factor)

        for j in (2, 0, 1):
            send_scale(2, c, j, dev_z(j))
            push(code_u.at[rows_of(c, at(z, j))], land_z.at[j, own(c)],
                 ssem.at[SUMZ], rsem.at[SUMZ, c], dev_z(j))

    def step4(c):
        receive_scale(2, c)
        receive(SUMZ, c, land_z.at[:, own(c)])

        @pl.loop(0, 4)
        def _(k):
            total = u[rows_of(c, z), unit_lanes(k)]
            for j in range(3):
                total = total + decode(2, j, c, land_z[j, own(c), unit_lanes(k)])
            sum_z[own(c), unit_lanes(k)] = total

        for j in (2, 0, 1):
            push(sum_z.at[own(c), unit_lanes(at(x, j))], land_x.at[j, own(c)],
                 ssem.at[SUMX], rsem.at[SUMX, c], dev_x(j))

    def step5(c):
        receive(SUMX, c, land_x.at[:, own(c)])
        total = sum_z[own(c), unit_lanes(x)]
        for j in range(3):
            total = total + land_x[j, own(c), :]
        where = rows_of(c, z)
        ob[where, :] = total
        for j in (2, 0, 1):
            push(ob.at[where], ob.at[where], ssem.at[AGZ], rsem.at[AGZ, c], dev_z(j))

    def step6(c):
        receive(AGZ, c, ob.at[own_rows(c, 3)])
        per = chunk // SCEN
        bound = ramp_limit[...][None]

        @pl.loop(0, per // 4)
        def _(k):
            h = c * per + k * 4
            step = gx[pl.ds(h + 1, 5)] - gx[pl.ds(h, 5)]
            dual = rw[pl.ds(h, 5)] * hinge_grad(step, bound)
            where = span(h * SCEN, 4 * SCEN)
            grad = ob[where, :].reshape(4, SCEN, n_units) + dual[:-1] - dual[1:]
            out[where, :] = (lev[pl.ds(h, 4)] * grad).reshape(4 * SCEN, n_units)

    def g_rows(h):
        return pl.ds(pl.multiple_of(h * HALF, HALF), HALF)

    def send_factor(j):
        where = pl.ds(pl.multiple_of(at(x, j) * QUARTER + hour * HALF, HALF), HALF)
        g_send[j] = jnp.dot(p[where, :], onehot[...], preferred_element_type=F32).astype(BF16)
        push(g_send.at[j], g.at[x, g_rows(hour)], g_sem.at[0], g_sem.at[1], dev_x(j))

    def own_factor():
        g[x] = jnp.dot(p[quarter(x), :], onehot[...], preferred_element_type=F32).astype(BF16)
        locals_in[3].wait()
        locals_in[4].wait()

        def ramps(k, carry):
            index = lax.rem(hour * hours + k, 2 * hours)
            inner = (index != 0).astype(F32)
            row = 2.0 * ramp_weight[...] * (ramp[pl.ds(index, 1), :].astype(F32) * inner)
            rw[k] = jnp.broadcast_to(row, (SCEN, n_units))
            return carry

        lax.fori_loop(0, hours + 1, ramps, 0)
        halo().wait()

    def share_factors():
        take(g_send, g_sem.at[1])
        for j in range(3):
            part = g.at[at(x, j), g_rows(hour)]
            push(part, part, g_sem.at[2], g_sem.at[3], sibling)

    def halo():
        return pltpu.make_async_remote_copy(
            src_ref=gx.at[hours - (hours - 1) * hour], dst_ref=gx.at[(hours + 1) * hour],
            send_sem=halo_sem.at[0], recv_sem=halo_sem.at[1], device_id=sibling, device_id_type=MESH,
        )

    rest_rows = pl.ds(block, columns - block)
    locals_in = [
        pltpu.make_async_copy(src, dst, in_sem.at[n])
        for n, (src, dst) in enumerate(
            [
                (commit_hbm, commit),
                (units_hbm, units),
                (load_hbm.at[pl.ds(0, block)], load.at[pl.ds(0, block)]),
                (active_hbm, active.at[:, pl.ds(0, lines)]),
                (ramp_hbm, ramp),
                (limit_hbm, lim.at[0, pl.ds(0, lines)]),
                (weight_hbm, wgt.at[0, pl.ds(0, lines)]),
                (load_hbm.at[rest_rows], load.at[rest_rows]),
            ]
        )
    ]
    for dma in locals_in[:2]:
        dma.start()
    fetch(lax.rem(x + 2, 4), lambda dma: dma.start())
    locals_in[2].start()
    barrier = pltpu.get_barrier_semaphore()
    for j in range(3):
        for dev in (dev_x(j), dev_y(j), dev_z(j)):
            pl.semaphore_signal(barrier, inc=1, device_id=dev, device_id_type=MESH)
    pl.semaphore_signal(barrier, inc=1, device_id=sibling, device_id_type=MESH)

    fill = 4 * QUARTER - lines
    p[lines:, :] = jnp.zeros((fill, nodes), BF16)
    onehot[...] = (
        lax.broadcasted_iota(jnp.int32, onehot.shape, 0) == node[...] - bus * nodes
    ).astype(F32).astype(BF16)
    gx[(hours + 1) * hour] = jnp.zeros((SCEN, n_units), F32)
    locals_in[0].wait()
    locals_in[1].wait()
    for k in range(1, 4):
        fetch(lax.rem(x + 2 + k, 4), lambda dma: dma.start())

    def generate(k, carry):
        row = commit[pl.ds(k, 1), :]
        value = jnp.zeros((1, n_units), F32)
        for n in range(levels.shape[0]):
            value = value + jnp.where(row == n, levels[n], 0.0)
        value = jnp.broadcast_to(value, (SCEN, n_units))
        lev[k] = value
        gx[k + 1] = value * units[k]
        return carry

    lax.fori_loop(0, block // SCEN, generate, 0)
    fetch(lax.rem(x + 2, 4), lambda dma: dma.wait())
    pl.semaphore_wait(barrier, 10)
    send_factor(2)
    locals_in[2].wait()

    steps = dict(
        F=forward, R=relay, Y=gather_relay,
        **dict(zip("123456", (step1, step2, step3, step4, step5, step6))),
    )

    def iteration(i, carry):
        for name, lag in ORDER:
            if name == "2":
                @pl.when(i == lag)
                def _():
                    locals_in[5].wait()
                    locals_in[6].wait()
            @pl.when((i >= lag) & (i < CHUNKS + lag))
            def _():
                steps[name](i - lag)

            if name == "F":
                @pl.when(i == 0)
                def _():
                    for n in (7, 3, 4, 5, 6):
                        locals_in[n].start()
                    lax.fori_loop(block // SCEN, hours, generate, 0)
                    halo().start()
                    active[:, lines:] = jnp.zeros((hours, fill), jnp.int32)
                    lim[:, lines:] = jnp.zeros((1, fill), F32)
                    wgt[:, lines:] = jnp.zeros((1, fill), F32)
                    own_factor()
                    locals_in[7].wait()

        for j in range(2):
            @pl.when(i == FACTORS[j])
            def _():
                send_factor(j)

        @pl.when(i == FACTORS[2])
        def _():
            share_factors()

        return carry

    lax.fori_loop(0, CHUNKS + max(lag for _, lag in ORDER), iteration, 0)
    take(part_a.at[pl.ds(0, 3)], ssem.at[OA])
    take(part_b.at[pl.ds(0, 3)], ssem.at[OB])
    for n in range(3):
        take(land_scale.at[n], ssem.at[SCALE + n])
    take(land2_a, ssem.at[S2A])
    take(land2_b, ssem.at[S2B])
    take(fg.at[pl.ds(0, 3 * (columns // 4))], ssem.at[AGY])
    take(land_z, ssem.at[SUMZ])
    take(land_x, ssem.at[SUMX])
    take(land_x, ssem.at[AGZ])
    take(g_send, g_sem.at[0])
    take(g_send, g_sem.at[2])


def body(
    ptdf, units_out, load, unit_node, commit_index, relax_levels,
    line_active, line_limit, line_weight, ramp_active, ramp_limit, ramp_weight,
):
    hours, scen, units = units_out.shape
    lines, nodes = ptdf.shape
    columns = hours * scen
    vmem = pl.BlockSpec(memory_space=pltpu.VMEM)
    smem = pl.BlockSpec(memory_space=pltpu.SMEM)
    anywhere = pl.BlockSpec(memory_space=pl.ANY)
    dma = pltpu.SemaphoreType.DMA
    all_lines = 4 * QUARTER
    own = columns // 4
    grad = pl.pallas_call(
        kernel,
        out_shape=jax.ShapeDtypeStruct((columns, units), F32),
        in_specs=[smem] + [anywhere] * 8 + [vmem] * 3,
        out_specs=vmem,
        scratch_shapes=[
            pltpu.VMEM((all_lines, nodes), BF16),
            pltpu.VMEM((columns, nodes), F32),
            pltpu.VMEM((hours, scen, units), F32),
            pltpu.VMEM((hours, units), jnp.int32),
            pltpu.VMEM((hours, all_lines), jnp.int32),
            pltpu.VMEM((2 * hours, units), jnp.int32),
            pltpu.VMEM((hours, scen, units), F32),
            pltpu.VMEM((hours + 2, scen, units), F32),
            pltpu.VMEM((hours + 1, scen, units), F32),
            pltpu.VMEM((1, all_lines), F32),
            pltpu.VMEM((1, all_lines), F32),
            pltpu.VMEM((columns // CHUNKS * TOGETHER, nodes), BF16),
            pltpu.VMEM((4, columns, SIDE_A), BF16),
            pltpu.VMEM((4, columns, SIDE_B), BF16),
            pltpu.VMEM((columns, SIDE_A), F32),
            pltpu.VMEM((columns, SIDE_A), F32),
            pltpu.VMEM((columns // CHUNKS * TOGETHER, SIDE_B), F32),
            pltpu.VMEM((4, own, SIDE_B), F32),
            pltpu.VMEM((4, own, SIDE_B), F32),
            pltpu.VMEM((columns, SIDE_A), BF16),
            pltpu.VMEM((4, own, SIDE_B), BF16),
            pltpu.VMEM((2, columns, SIDE_A), BF16),
            pltpu.VMEM((2, 4, own, SIDE_B), BF16),
            pltpu.VMEM((columns // CHUNKS, SIDE_A), F32),
            pltpu.VMEM((columns // CHUNKS, SIDE_B), F32),
            pltpu.VMEM((columns, SIDE_A), jnp.int16),
            pltpu.VMEM((4, own, SIDE_B), jnp.int16),
            pltpu.VMEM((3, own, SIDE_A), jnp.int16),
            pltpu.VMEM((3, own, SIDE_B), jnp.int16),
            pltpu.VMEM((3, CHUNKS, 8, 128), F32),
            pltpu.VMEM((3, 3, CHUNKS, 8, 128), F32),
            pltpu.VMEM((columns, QUARTER), BF16),
            pltpu.VMEM((columns, 4 * units), F32),
            pltpu.VMEM((columns, 4 * units), jnp.int16),
            pltpu.VMEM((3, own, 4 * units), jnp.int16),
            pltpu.VMEM((own, 4 * units), F32),
            pltpu.VMEM((3, own, units), F32),
            pltpu.VMEM((columns, units), F32),
            pltpu.VMEM((nodes, units), BF16),
            pltpu.VMEM((3, HALF, units), BF16),
            pltpu.VMEM((4, QUARTER, units), BF16),
            dma((4,)),
            dma((8,)),
            dma((KINDS,)),
            dma((KINDS, CHUNKS)),
            dma((4,)),
            dma((2,)),
        ],
        compiler_params=pltpu.CompilerParams(
            collective_id=0, has_side_effects=True, vmem_limit_bytes=63 << 20
        ),
    )(
        relax_levels, ptdf, load.reshape(columns, nodes), units_out, commit_index, line_active,
        ramp_active, line_limit, line_weight, unit_node[None, :], ramp_limit[None, :],
        ramp_weight[None, :],
    )
    return grad.reshape(hours, scen, units)


def solution(mesh):
    return jax.shard_map(
        body,
        mesh=mesh,
        in_specs=(
            P("line", "bus"),
            P("hour", None, "bus"),
            P("hour", None, "bus"),
            P("bus"),
            P("hour", "bus"),
            P(),
            P("hour", "line"),
            P("line"),
            P("line"),
            P(None, "bus"),
            P("bus"),
            P("bus"),
        ),
        out_specs=P("hour", None, "bus"),
        check_vma=False,
    )
```
